1024 devices in a mesh: space: 32 (over y, z_lo), chan: 8 (over x, core), filt: 4 (over z_hi).
Axes of the slice: x: 4, y: 4, z: 32 (z_hi: 4, z_lo: 8; z = z_hi * 8 + z_lo), core: 2. Of those that a mesh axis runs over, the one named last changes fastest.
Arguments:
- activations: bfloat16 [256, 128, 4, 128], P('chan', 'space'), may hold values from -6 to 6
- out_grad: bfloat16 [4, 64, 128, 4, 128], P('filt', 'chan', 'space'), may hold values from -6 to 6
- weight: bfloat16 [27, 256, 256], P(None, 'chan', 'filt'), may hold values from -0.078125 to 0.078125
Outputs:
- grad_input: bfloat16 [256, 128, 4, 128], P(('chan', 'filt'), 'space')
- grad_weight: float32 [27, 256, 256], P(None, 'chan', 'filt')
The draws below stay inside these ranges and needn't reach their ends.
All inputs are finite; a program needn't handle non-finite values.
Results may differ from the reference program's by a relative error of at most 0.001.
Values may be sent and summed in bfloat16 or wider, within the bound.
A program may use at most 32 MiB of HBM per device.

```python
import math
import jax
import jax.numpy as jnp
from jax import lax

CIN = 256
COUT = 256
Y = 128
Z = 4
X = 128
N_FILT = 4


def steps_of(stream_key, dims, cuts, low, largest):
    factor_of, own = 1.0, jax.random.fold_in(stream_key, 6)
    for axis_at, blocks in cuts:
        heights = jnp.exp(jax.random.uniform(jax.random.fold_in(own, axis_at), (blocks,), jnp.float32, low / len(cuts), largest / len(cuts)))
        factor_of = factor_of * jnp.repeat(heights, dims[axis_at] // blocks).reshape([-1 if axis == axis_at else 1 for axis in range(len(dims))])
    return factor_of


def bell_draw(key, dims, width, most, shards=(), dtype=jnp.bfloat16):
    values = width * jax.random.normal(key, dims, jnp.float32)
    if shards:
        values = values * steps_of(key, dims, shards, -0.22, 0.18)
    return jnp.clip(values, -most, most).astype(dtype)


def setup_inputs(seed: int = 0) -> dict:
    keys = jax.random.split(jax.random.key(seed), 4)
    activations = bell_draw(keys[0], (CIN, X, Z, Y), 1.0, 6.0, ((0, 8), (1, 32)))
    out_grad = bell_draw(keys[1], (N_FILT, COUT // N_FILT, X, Z, Y), 1.0, 6.0, ((0, 4), (1, 8), (2, 32)))
    weight = bell_draw(keys[2], (27, CIN, COUT), (27 * CIN) ** -0.5, 0.078125, ((1, 8), (2, 4)))
    return dict(activations=activations, out_grad=out_grad, weight=weight)


def reference(activations, out_grad, weight):
    chan_in = activations.shape[0]
    blocks_f, block, count_x, count_z, count_y = out_grad.shape
    chan_out = blocks_f * block
    cells = count_x * count_y * count_z
    act_xyz = jnp.transpose(activations, (1, 3, 2, 0))
    grad_xyz = jnp.transpose(out_grad.reshape(chan_out, count_x, count_z, count_y), (1, 3, 2, 0))
    padded = jnp.pad(grad_xyz.astype(jnp.float32), ((1, 1), (1, 1), (1, 1), (0, 0)))
    flat_act = act_xyz.astype(jnp.float32).reshape(cells, chan_in)
    weight_full = weight.astype(jnp.float32)
    total = jnp.zeros((cells, chan_in), jnp.float32)
    tap_blocks = [[] for tap_index in range(27)]
    for block_index in range(blocks_f):
        low = block_index * block
        part = jnp.zeros((cells, chan_in), jnp.float32)
        for shift_x in range(3):
            for shift_y in range(3):
                for shift_z in range(3):
                    tap_index = (shift_x * 3 + shift_y) * 3 + shift_z
                    shifted = padded[2 - shift_x:2 - shift_x + count_x, 2 - shift_y:2 - shift_y + count_y, 2 - shift_z:2 - shift_z + count_z, low:low + block].reshape(cells, block)
                    part = part + jnp.dot(shifted, weight_full[tap_index, :, low:low + block].T, precision=lax.Precision.HIGHEST)
                    tap_blocks[tap_index].append(jnp.dot(flat_act.T, shifted, precision=lax.Precision.HIGHEST))
        total = total + part
    grad_input = total.astype(jnp.bfloat16).reshape(count_x, count_y, count_z, chan_in)
    grad_input = jnp.transpose(grad_input, (3, 0, 2, 1))
    grad_weight = jnp.stack([jnp.concatenate(pieces, axis=1) for pieces in tap_blocks], axis=0)
    grad_weight = grad_weight * jnp.float32(1.0 / math.sqrt(cells))
    return (grad_input, grad_weight)
```

```python
import functools
import math

import jax
import jax.numpy as jnp
from jax import lax
from jax.experimental import pallas as pl
from jax.experimental.pallas import tpu as pltpu
from jax.sharding import PartitionSpec as P

MESH = pl.DeviceIdType.MESH
F32, BF16 = jnp.float32, jnp.bfloat16
ROWS = 512
TAP_ROWS = 128


def kernel(
    sizes, scale,
    act_ref, shard_ref, taps_ref,
    gi_ref, gw_ref,
    grads, acts, wparts, lhs, acc, mine, from_y, for_z, from_z, total, prod, outs, halo,
    s_own, r_own, s_act, r_act, s_filt, r_filt, s_wf, r_wf, s_wy, r_wy, s_x, r_x, s_sib, r_sib,
    s_yr, r_yr, s_zr, r_zr, s_zg, r_zg, s_yg, r_yg, s_halo, r_halo,
):
    ny, nz, nx, nf = sizes
    nc, ns = nx * 2, ny * nz
    space, chan, filt = lax.axis_index("space"), lax.axis_index("chan"), lax.axis_index("filt")
    row, run = space // nz, space % nz
    chip, core = chan // 2, chan % 2
    sib = chip * 2 + (1 - core)
    shard_rows = shard_ref.shape[0]
    own_filt = shard_rows // 16
    y_rows = ROWS // ny
    z_rows = y_rows // nz
    w_rows = TAP_ROWS // ny
    before, after = (space + ns - 1) % ns, (space + 1) % ns

    def at_y(d):
        return {"space": ((row + d) % ny) * nz + run}

    def at_z(d):
        return {"space": row * nz + (run + d) % nz}

    def at_x(d):
        return {"chan": ((chip + d) % nx) * 2 + core}

    barrier = pltpu.get_barrier_semaphore()
    partners = [{"chan": (chan + d) % nc} for d in range(1, nc)]
    partners += [{"filt": (filt + d) % nf} for d in range(1, nf)]
    partners += [at_y(d) for d in range(1, ny)] + [at_z(d) for d in range(1, nz)]
    partners += [{"space": before}, {"space": after}]
    for partner in partners:
        pl.semaphore_signal(barrier, inc=1, device_id=partner, device_id_type=MESH)

    sent = []

    def remote(src, dst, ssem, rsem, where):
        copy = pltpu.make_async_remote_copy(
            src_ref=src, dst_ref=dst, send_sem=ssem, recv_sem=rsem, device_id=where, device_id_type=MESH
        )
        copy.start()
        sent.append(copy)
        return copy

    grads[0, chan] = shard_ref[...]
    empty = jnp.zeros((6, 32, 128), BF16)
    acts[:, 0] = empty
    acts[:, 5] = empty
    acts[1:5, 1:5] = act_ref[...]
    acc[...] = jnp.zeros(acc.shape, F32)
    pl.semaphore_wait(barrier, len(partners))

    own = [
        remote(shard_ref, grads.at[0, chan], s_own.at[d - 1], r_own.at[d - 1], {"chan": (chan + d) % nc})
        for d in range(1, nc)
    ]
    up = remote(act_ref.at[3], acts.at[0, pl.ds(1, 4)], s_act.at[0], r_act.at[0], {"space": after})
    down = remote(act_ref.at[0], acts.at[5, pl.ds(1, 4)], s_act.at[1], r_act.at[1], {"space": before})
    over = {}
    for d in range(1, nf):
        over[d] = remote(
            shard_ref, grads.at[d, chan], s_filt.at[d - 1], r_filt.at[d - 1], {"filt": (filt + d) % nf}
        )
    wover = {}
    for d in range(1, nf):
        target = (filt + d) % nf
        wover[d] = remote(
            taps_ref.at[target, pl.ds(pl.multiple_of(row * w_rows, w_rows), w_rows)],
            wparts.at[row, d - 1], s_wf.at[d - 1], r_wf.at[d - 1], {"filt": target},
        )

    rim = jnp.zeros((6, 256, 128), F32)
    for x in (0, 1, 6, 7):
        prod[x] = rim
    for x in range(2, 6):
        prod[x, 0] = rim[0]
        prod[x, 5] = rim[0]

    lane = lax.broadcasted_iota(jnp.int32, (1, 128), 1)
    first, last = lane == 0, lane == 127

    for copy in own:
        copy.wait_recv()
    up.wait_recv()
    down.wait_recv()
    zero = jnp.zeros((4, 32, 128), BF16)
    acts[0, 1:5] = jnp.where(space > 0, acts[0, 1:5], zero)
    acts[5, 1:5] = jnp.where(space < ns - 1, acts[5, 1:5], zero)

    def pair_of(block):
        parts = block.astype(F32).reshape(-1, 2, own_filt, 128)
        return [parts[:, i].reshape(-1, 128) for i in range(2)]

    def taps_step(h, carry):
        x, z = h // 2, (h % 2) * 2
        start = pl.multiple_of(h * 2 * own_filt, 2 * own_filt)
        columns = []
        for g in pair_of(grads[0, :, pl.ds(start, 2 * own_filt), :]):
            low = jnp.where(last, 0.0, pltpu.roll(g, 127, 1))
            high = jnp.where(first, 0.0, pltpu.roll(g, 1, 1))
            columns.append(jnp.concatenate([low, g, high], axis=0).astype(BF16))
        rhs = jnp.concatenate(columns, axis=1)
        halves = [
            jnp.concatenate([acts[x + a, z + c + i] for a in range(3) for c in range(3)], axis=0)
            for i in range(2)
        ]
        acc[:, 0:192] += lax.dot_general(
            jnp.concatenate(halves, axis=1), rhs, (((1,), (1,)), ((), ())), preferred_element_type=F32
        )
        return carry

    lax.fori_loop(0, 8, taps_step, 0)
    mine[0:288] = acc[:, 0:128] * scale
    third = acc[:, 128:256] * scale
    mine[288:432] = jnp.where(lane < 64, third[0:144], pltpu.roll(third[144:288], 64, 1))
    mine[432:512] = jnp.zeros((80, 128), F32)

    y_red = []
    for d in range(1, ny):
        theirs = pl.multiple_of((row + d) % ny * y_rows, y_rows)
        y_red.append(
            remote(mine.at[pl.ds(theirs, y_rows)], from_y.at[d - 1], s_yr.at[d - 1], r_yr.at[d - 1], at_y(d))
        )

    x_copies, sib_copies = {}, {}

    def forward(d):
        over[d].wait_recv()
        for e in range(1, nx):
            x_copies[d, e] = remote(
                grads.at[d, chan], grads.at[d, chan], s_x.at[d - 1, e - 1], r_x.at[d - 1, e - 1], at_x(e)
            )
        sib_copies[d, 0] = remote(
            grads.at[d, chan], grads.at[d, chan], s_sib.at[d - 1, 0], r_sib.at[d - 1, 0], {"chan": sib}
        )

    def share(d):
        for e in range(1, nx):
            x_copies[d, e].wait_recv()
            source = ((chip + nx - e) % nx) * 2 + core
            sib_copies[d, e] = remote(
                grads.at[d, source], grads.at[d, source], s_sib.at[d - 1, e], r_sib.at[d - 1, e], {"chan": sib}
            )

    forward(1)
    forward(3)

    mine_y = pl.multiple_of(row * y_rows, y_rows)
    for copy in y_red:
        copy.wait_recv()
    part = mine[pl.ds(mine_y, y_rows)]
    for d in range(1, ny):
        part = part + from_y[d - 1]
    for_z[...] = part
    z_red = []
    for d in range(1, nz):
        theirs = pl.multiple_of((run + d) % nz * z_rows, z_rows)
        z_red.append(
            remote(for_z.at[pl.ds(theirs, z_rows)], from_z.at[d - 1], s_zr.at[d - 1], r_zr.at[d - 1], at_z(d))
        )

    for d in range(1, nf):
        wover[d].wait_recv()
    wshare = [
        remote(wparts.at[row], wparts.at[row], s_wy.at[d - 1], r_wy.at[d - 1], at_y(d)) for d in range(1, ny)
    ]
    forward(2)
    share(1)
    share(3)

    for copy in z_red:
        copy.wait_recv()
    part = for_z[pl.ds(pl.multiple_of(run * z_rows, z_rows), z_rows)]
    for d in range(1, nz):
        part = part + from_z[d - 1]
    place = pl.ds(pl.multiple_of(mine_y + run * z_rows, z_rows), z_rows)
    total[place] = part
    z_gat = [
        remote(total.at[place], total.at[place], s_zg.at[d - 1], r_zg.at[d - 1], at_z(d)) for d in range(1, nz)
    ]
    share(2)

    for copy in wshare:
        copy.wait_recv()
    blocks = [taps_ref[filt].astype(F32)]
    blocks += [wparts[:, d].reshape(TAP_ROWS, 128).astype(F32) for d in range(nf - 1)]
    for i in range(0, nf, 2):
        a, b = blocks[i], blocks[i + 1]
        lhs[0:128, i * 64 : i * 64 + 128] = jnp.where(lane < 64, a, pltpu.roll(b, 64, 1)).astype(BF16)
        lhs[128:256, i * 64 : i * 64 + 128] = jnp.where(lane < 64, pltpu.roll(a, 64, 1), b).astype(BF16)

    for copy in z_gat:
        copy.wait_recv()
    place_y = pl.ds(mine_y, y_rows)
    y_gat = [
        remote(total.at[place_y], total.at[place_y], s_yg.at[d - 1], r_yg.at[d - 1], at_y(d)) for d in range(1, ny)
    ]

    for copy in sib_copies.values():
        copy.wait_recv()

    def prod_step(h, carry):
        x, z = h // 2, (h % 2) * 2
        start = pl.multiple_of(h * 2 * own_filt, 2 * own_filt)
        block = grads[:, :, pl.ds(start, 2 * own_filt), :].reshape(nf * nc, 2 * own_filt, 128)
        rhs = jnp.concatenate(pair_of(block), axis=1).astype(BF16)
        result = jnp.dot(lhs[...], rhs, preferred_element_type=F32)
        prod[x + 2, z + 1] = result[:, :128]
        prod[x + 2, z + 2] = result[:, 128:]
        return carry

    lax.fori_loop(0, 8, prod_step, 0)

    def sum_step(n, x):
        z = n
        sums = []
        for b in range(3):
            terms = []
            for a in range(3):
                for c in range(3):
                    k = (a * 3 + b) * 3 + c
                    at = (k % 2) * 128 + (k // 2) * 8
                    terms.append(prod[x + 2 - a, z + 2 - c, at : at + 8])
            sums.append(functools.reduce(jnp.add, terms))
        low = jnp.where(last, 0.0, pltpu.roll(sums[0], 127, 1))
        high = jnp.where(first, 0.0, pltpu.roll(sums[2], 1, 1))
        outs[x, z] = sums[1] + low + high
        return x

    def layer(x):
        for n in range(4):
            sum_step(n, x)

    layer(0)
    low_out = remote(outs.at[0], halo.at[1], s_halo.at[0], r_halo.at[0], {"space": before})
    layer(5)
    high_out = remote(outs.at[5], halo.at[0], s_halo.at[1], r_halo.at[1], {"space": after})

    def inner(x, carry):
        layer(x)
        return carry

    lax.fori_loop(1, 5, inner, 0)

    for copy in y_gat:
        copy.wait_recv()
    for a in range(3):
        for c in range(3):
            block = (a * 3 + c) * 32
            for b in range(2):
                gw_ref[(a * 3 + b) * 3 + c] = total[block : block + 32, b * 64 : b * 64 + 64]
            for half in range(2):
                at = block + half * 16
                left = 0 if at < 144 else 64
                src = 288 + (at if at < 144 else at - 144)
                gw_ref[(a * 3 + 2) * 3 + c, half * 16 : half * 16 + 16] = total[src : src + 16, left : left + 64]

    low_out.wait_recv()
    high_out.wait_recv()
    outs[1] = outs[1] + jnp.where(space > 0, halo[0], 0.0)
    outs[4] = outs[4] + jnp.where(space < ns - 1, halo[1], 0.0)
    gi_ref[...] = outs[1:5].reshape(128, 128).astype(BF16)
    for copy in sent:
        copy.wait_send()


def body(sizes, activations, out_grad, weight):
    ny, nz, nx, nf = sizes
    nc = nx * 2
    act = jnp.transpose(activations, (1, 2, 0, 3))
    own_filt = out_grad.shape[1]
    shard = jnp.transpose(out_grad[0], (1, 2, 0, 3)).reshape(16 * own_filt, 128)
    taps = jnp.pad(weight, ((0, 5), (0, 0), (0, 0))).reshape(16, 2, nf, 8, 64)
    taps = jnp.transpose(taps, (2, 0, 3, 1, 4)).reshape(nf, TAP_ROWS, 128)
    cells = 16 * 128 * ny * nz
    dma = pltpu.SemaphoreType.DMA
    vmem = pl.BlockSpec(memory_space=pltpu.VMEM)
    y_rows = ROWS // ny
    z_rows = y_rows // nz
    pairs = []
    for shape in (
        (nc - 1,), (2,), (nf - 1,), (nf - 1,), (ny - 1,), (nf - 1, max(nx - 1, 1)), (nf - 1, nx),
        (ny - 1,), (nz - 1,), (nz - 1,), (ny - 1,), (2,),
    ):
        pairs += [dma(shape), dma(shape)]
    gi, gw = pl.pallas_call(
        functools.partial(kernel, sizes, 1.0 / math.sqrt(cells)),
        out_shape=(
            jax.ShapeDtypeStruct((128, 128), BF16),
            jax.ShapeDtypeStruct((27, 32, 64), F32),
        ),
        in_specs=[vmem] * 3,
        out_specs=(vmem, vmem),
        scratch_shapes=[
            pltpu.VMEM((nf, nc, 16 * own_filt, 128), BF16),
            pltpu.VMEM((6, 6, 32, 128), BF16),
            pltpu.VMEM((ny, nf - 1, TAP_ROWS // ny, 128), BF16),
            pltpu.VMEM((256, 256), BF16),
            pltpu.VMEM((288, 256), F32),
            pltpu.VMEM((ROWS, 128), F32),
            pltpu.VMEM((ny - 1, y_rows, 128), F32),
            pltpu.VMEM((y_rows, 128), F32),
            pltpu.VMEM((nz - 1, z_rows, 128), F32),
            pltpu.VMEM((ROWS, 128), F32),
            pltpu.VMEM((8, 6, 256, 128), F32),
            pltpu.VMEM((6, 4, 8, 128), F32),
            pltpu.VMEM((2, 4, 8, 128), F32),
        ] + pairs,
        compiler_params=pltpu.CompilerParams(
            collective_id=0, has_side_effects=True, vmem_limit_bytes=32 * 1024 * 1024
        ),
    )(act, shard, taps)
    return jnp.transpose(gi.reshape(4, 4, 8, 128), (2, 0, 1, 3)), gw


def solution(mesh):
    ns = mesh.shape["space"]
    nz = 8 if ns % 8 == 0 else 2
    sizes = (ns // nz, nz, mesh.shape["chan"] // 2, mesh.shape["filt"])
    return jax.shard_map(
        functools.partial(body, sizes),
        mesh=mesh,
        in_specs=(
            P("chan", "space", None, None),
            P("filt", "chan", "space", None, None),
            P(None, "chan", "filt"),
        ),
        out_specs=(P(("chan", "filt"), "space", None, None), P(None, "chan", "filt")),
        check_vma=False,
    )
```

```python
import functools
import math

import jax
import jax.numpy as jnp
from jax import lax
from jax.experimental import pallas as pl
from jax.experimental.pallas import tpu as pltpu
from jax.sharding import PartitionSpec as P

MESH = pl.DeviceIdType.MESH
F32, BF16 = jnp.float32, jnp.bfloat16
ROWS = 512
TAP_ROWS = 128


def kernel(
    sizes, scale,
    act_hbm, shard_hbm, weight_hbm,
    gi_ref, gw_ref,
    act_raw, shard_raw, weight_raw, act_stage, shard_stage, shard_ref, taps_ref, in_sems, told,
    grads, acts, wparts, lhs, acc, mine, from_y, for_z, from_z, total, prod, outs, halo,
    s_own, r_own, s_act, r_act, s_filt, r_filt, s_wf, r_wf, s_wy, r_wy, s_x, r_x, s_sib, r_sib,
    s_yr, r_yr, s_zr, r_zr, s_zg, r_zg, s_yg, r_yg, s_halo, r_halo,
):
    ny, nz, nx, nf = sizes
    nc, ns = nx * 2, ny * nz
    space, chan, filt = lax.axis_index("space"), lax.axis_index("chan"), lax.axis_index("filt")
    row, run = space // nz, space % nz
    chip, core = chan // 2, chan % 2
    sib = chip * 2 + (1 - core)
    shard_rows = shard_ref.shape[0]
    own_filt = shard_rows // 16
    y_rows = ROWS // ny
    z_rows = y_rows // nz
    w_rows = TAP_ROWS // ny
    before, after = (space + ns - 1) % ns, (space + 1) % ns

    def at_y(d):
        return {"space": ((row + d) % ny) * nz + run}

    def at_z(d):
        return {"space": row * nz + (run + d) % nz}

    def at_x(d):
        return {"chan": ((chip + d) % nx) * 2 + core}

    rank = jnp.where(filt < 2, filt, 5 - filt)

    def filt_at(d):
        target = (filt + d) % nf
        return target, jnp.where(target < 2, target, 5 - target)

    barrier = pltpu.get_barrier_semaphore()
    partners = [{"chan": (chan + d) % nc} for d in range(1, nc)]
    partners += [at_y(d) for d in range(1, ny)] + [at_z(d) for d in range(1, nz)]
    partners += [{"space": before}, {"space": after}]
    for partner in partners:
        pl.semaphore_signal(barrier, inc=1, device_id=partner, device_id_type=MESH)
    for d in range(1, nf):
        target, target_rank = filt_at(d)

        @pl.when(rank < target_rank)
        def _(target=target):
            pl.semaphore_signal(barrier, inc=1, device_id={"filt": target}, device_id_type=MESH)

    loads = [
        pltpu.make_async_copy(src, dst, in_sems.at[n])
        for n, (src, dst) in enumerate(((shard_hbm, shard_raw), (act_hbm, act_raw), (weight_hbm, weight_raw)))
    ]
    for load in loads:
        load.start()

    sent = []

    def remote(src, dst, ssem, rsem, where, start=True):
        copy = pltpu.make_async_remote_copy(
            src_ref=src, dst_ref=dst, send_sem=ssem, recv_sem=rsem, device_id=where, device_id_type=MESH
        )
        if start:
            copy.start()
        sent.append(copy)
        return copy

    lane = lax.broadcasted_iota(jnp.int32, (1, 128), 1)
    first, last = lane == 0, lane == 127
    loads[0].wait()
    for o in range(own_filt):
        shard_stage[:, :, o, :] = shard_raw[0, o].astype(F32)
    shard_ref[...] = shard_stage[...].reshape(shard_rows, 128).astype(BF16)
    grads[0, chan] = shard_ref[...]
    loads[1].wait()
    for i in range(32):
        act_stage[:, :, i, :] = act_raw[i].astype(F32)
    acts[1:5, 1:5] = act_stage[...].astype(BF16)
    empty = jnp.zeros((6, 32, 128), BF16)
    acts[:, 0] = empty
    acts[:, 5] = empty
    loads[2].wait()
    blank = jnp.zeros((8, 64), F32)
    for block in range(nf):
        pieces = []
        for k in range(0, 32, 2):
            pair = [
                weight_raw[t].astype(F32)[block * 8 : block * 8 + 8] if t < 27 else blank for t in (k, k + 1)
            ]
            pieces.append(jnp.concatenate(pair, axis=1))
        taps_ref[block] = jnp.concatenate(pieces, axis=0).astype(BF16)
    acc[...] = jnp.zeros(acc.shape, F32)
    pl.semaphore_wait(barrier, len(partners) + rank)

    over, wover = {}, {}
    for d in range(1, nf):
        target, target_rank = filt_at(d)
        over[d] = remote(
            shard_ref, grads.at[d, chan], s_filt.at[d - 1], r_filt.at[d - 1], {"filt": target}, start=False
        )
        wover[d] = remote(
            taps_ref.at[target, pl.ds(pl.multiple_of(row * w_rows, w_rows), w_rows)],
            wparts.at[row, d - 1], s_wf.at[d - 1], r_wf.at[d - 1], {"filt": target}, start=False,
        )

    def send_back(d):
        target, target_rank = filt_at(d)

        @pl.when(rank > target_rank)
        def _():
            pl.semaphore_signal(told.at[d - 1], inc=1, device_id={"filt": target}, device_id_type=MESH)
            over[d].start()
            wover[d].start()

    def send_on(d, who):
        target, target_rank = filt_at(d)

        @pl.when(functools.reduce(jnp.logical_or, [filt == w for w in who]))
        def _():
            pl.semaphore_wait(told.at[nf - d - 1], 1)
            over[d].start()
            wover[d].start()

    send_back(2)
    send_back(1)
    send_back(3)
    own = [
        remote(shard_ref, grads.at[0, chan], s_own.at[d - 1], r_own.at[d - 1], {"chan": (chan + d) % nc})
        for d in range(1, nc)
    ]
    up = remote(acts.at[4, pl.ds(1, 4)], acts.at[0, pl.ds(1, 4)], s_act.at[0], r_act.at[0], {"space": after})
    down = remote(acts.at[1, pl.ds(1, 4)], acts.at[5, pl.ds(1, 4)], s_act.at[1], r_act.at[1], {"space": before})

    rim = jnp.zeros((6, 256, 128), F32)
    for x in (0, 1, 6, 7):
        prod[x] = rim
    for x in range(2, 6):
        prod[x, 0] = rim[0]
        prod[x, 5] = rim[0]

    for copy in own:
        copy.wait_recv()
    up.wait_recv()
    down.wait_recv()
    zero = jnp.zeros((4, 32, 128), BF16)
    acts[0, 1:5] = jnp.where(space > 0, acts[0, 1:5], zero)
    acts[5, 1:5] = jnp.where(space < ns - 1, acts[5, 1:5], zero)

    def pair_of(block):
        parts = block.astype(F32).reshape(-1, 2, own_filt, 128)
        return [parts[:, i].reshape(-1, 128) for i in range(2)]

    def taps_step(h, carry):
        x, z = h // 2, (h % 2) * 2
        start = pl.multiple_of(h * 2 * own_filt, 2 * own_filt)
        columns = []
        for g in pair_of(grads[0, :, pl.ds(start, 2 * own_filt), :]):
            low = jnp.where(last, 0.0, pltpu.roll(g, 127, 1))
            high = jnp.where(first, 0.0, pltpu.roll(g, 1, 1))
            columns.append(jnp.concatenate([low, g, high], axis=0).astype(BF16))
        rhs = jnp.concatenate(columns, axis=1)
        halves = [
            jnp.concatenate([acts[x + a, z + c + i] for a in range(3) for c in range(3)], axis=0)
            for i in range(2)
        ]
        acc[:, 0:192] += lax.dot_general(
            jnp.concatenate(halves, axis=1), rhs, (((1,), (1,)), ((), ())), preferred_element_type=F32
        )
        return carry

    lax.fori_loop(0, 8, taps_step, 0)
    mine[0:288] = acc[:, 0:128] * scale
    third = acc[:, 128:256] * scale
    mine[288:432] = jnp.where(lane < 64, third[0:144], pltpu.roll(third[144:288], 64, 1))
    mine[432:512] = jnp.zeros((80, 128), F32)

    y_red = []
    for d in range(1, ny):
        theirs = pl.multiple_of((row + d) % ny * y_rows, y_rows)
        y_red.append(
            remote(mine.at[pl.ds(theirs, y_rows)], from_y.at[d - 1], s_yr.at[d - 1], r_yr.at[d - 1], at_y(d))
        )

    x_copies, sib_copies = {}, {}

    def forward(d):
        over[d].wait_recv()
        for e in range(1, nx):
            x_copies[d, e] = remote(
                grads.at[d, chan], grads.at[d, chan], s_x.at[d - 1, e - 1], r_x.at[d - 1, e - 1], at_x(e)
            )
        sib_copies[d, 0] = remote(
            grads.at[d, chan], grads.at[d, chan], s_sib.at[d - 1, 0], r_sib.at[d - 1, 0], {"chan": sib}
        )

    def share(d):
        for e in range(1, nx):
            x_copies[d, e].wait_recv()
            source = ((chip + nx - e) % nx) * 2 + core
            sib_copies[d, e] = remote(
                grads.at[d, source], grads.at[d, source], s_sib.at[d - 1, e], r_sib.at[d - 1, e], {"chan": sib}
            )

    send_on(1, (1,))
    send_on(3, (3,))
    send_on(2, (1,))

    mine_y = pl.multiple_of(row * y_rows, y_rows)
    for copy in y_red:
        copy.wait_recv()
    part = mine[pl.ds(mine_y, y_rows)]
    for d in range(1, ny):
        part = part + from_y[d - 1]
    for_z[...] = part
    z_red = []
    for d in range(1, nz):
        theirs = pl.multiple_of((run + d) % nz * z_rows, z_rows)
        z_red.append(
            remote(for_z.at[pl.ds(theirs, z_rows)], from_z.at[d - 1], s_zr.at[d - 1], r_zr.at[d - 1], at_z(d))
        )

    send_on(1, (0,))
    send_on(3, (0,))
    forward(1)
    forward(3)

    for copy in z_red:
        copy.wait_recv()
    part = for_z[pl.ds(pl.multiple_of(run * z_rows, z_rows), z_rows)]
    for d in range(1, nz):
        part = part + from_z[d - 1]
    place = pl.ds(pl.multiple_of(mine_y + run * z_rows, z_rows), z_rows)
    total[place] = part
    z_gat = [
        remote(total.at[place], total.at[place], s_zg.at[d - 1], r_zg.at[d - 1], at_z(d)) for d in range(1, nz)
    ]
    send_on(2, (0,))
    share(1)
    share(3)
    for d in range(1, nf):
        wover[d].wait_recv()
    wshare = [
        remote(wparts.at[row], wparts.at[row], s_wy.at[d - 1], r_wy.at[d - 1], at_y(d)) for d in range(1, ny)
    ]
    forward(2)

    for copy in wshare:
        copy.wait_recv()
    blocks = [taps_ref[filt].astype(F32)]
    blocks += [wparts[:, d].reshape(TAP_ROWS, 128).astype(F32) for d in (0, 2, 1)]
    for i in range(0, nf, 2):
        a, b = blocks[i], blocks[i + 1]
        lhs[0:128, i * 64 : i * 64 + 128] = jnp.where(lane < 64, a, pltpu.roll(b, 64, 1)).astype(BF16)
        lhs[128:256, i * 64 : i * 64 + 128] = jnp.where(lane < 64, pltpu.roll(a, 64, 1), b).astype(BF16)

    share(2)
    for copy in z_gat:
        copy.wait_recv()
    place_y = pl.ds(mine_y, y_rows)
    y_gat = [
        remote(total.at[place_y], total.at[place_y], s_yg.at[d - 1], r_yg.at[d - 1], at_y(d)) for d in range(1, ny)
    ]

    def product(which, columns, add):
        def step(h, carry):
            x, z = h // 2, (h % 2) * 2
            start = pl.multiple_of(h * 2 * own_filt, 2 * own_filt)
            parts = [pair_of(grads[d, :, pl.ds(start, 2 * own_filt), :]) for d in which]
            rhs = jnp.concatenate(
                [jnp.concatenate([p[i] for p in parts], axis=0) for i in range(2)], axis=1
            ).astype(BF16)
            result = jnp.dot(lhs[:, columns], rhs, preferred_element_type=F32)
            for i in range(2):
                half = result[:, i * 128 : i * 128 + 128]
                prod[x + 2, z + 1 + i] = prod[x + 2, z + 1 + i] + half if add else half
            return carry

        lax.fori_loop(0, 8, step, 0)

    for (d, e), copy in sib_copies.items():
        if d != 2:
            copy.wait_recv()
    product((0, 1, 3), slice(0, 192), False)
    for (d, e), copy in sib_copies.items():
        if d == 2:
            copy.wait_recv()
    product((2,), slice(192, 256), True)

    def sum_step(n, x):
        z = n
        sums = []
        for b in range(3):
            terms = []
            for a in range(3):
                for c in range(3):
                    k = (a * 3 + b) * 3 + c
                    at = (k % 2) * 128 + (k // 2) * 8
                    terms.append(prod[x + 2 - a, z + 2 - c, at : at + 8])
            sums.append(functools.reduce(jnp.add, terms))
        low = jnp.where(last, 0.0, pltpu.roll(sums[0], 127, 1))
        high = jnp.where(first, 0.0, pltpu.roll(sums[2], 1, 1))
        outs[x, z] = sums[1] + low + high
        return x

    def layer(x):
        for n in range(4):
            sum_step(n, x)

    layer(0)
    low_out = remote(outs.at[0], halo.at[1], s_halo.at[0], r_halo.at[0], {"space": before})
    layer(5)
    high_out = remote(outs.at[5], halo.at[0], s_halo.at[1], r_halo.at[1], {"space": after})

    def inner(x, carry):
        layer(x)
        return carry

    lax.fori_loop(1, 5, inner, 0)

    for copy in y_gat:
        copy.wait_recv()
    for a in range(3):
        for c in range(3):
            block = (a * 3 + c) * 32
            for b in range(2):
                gw_ref[(a * 3 + b) * 3 + c] = total[block : block + 32, b * 64 : b * 64 + 64]
            for half in range(2):
                at = block + half * 16
                left = 0 if at < 144 else 64
                src = 288 + (at if at < 144 else at - 144)
                gw_ref[(a * 3 + 2) * 3 + c, half * 16 : half * 16 + 16] = total[src : src + 16, left : left + 64]

    low_out.wait_recv()
    high_out.wait_recv()
    outs[1] = outs[1] + jnp.where(space > 0, halo[0], 0.0)
    outs[4] = outs[4] + jnp.where(space < ns - 1, halo[1], 0.0)
    gi_ref[...] = outs[1:5].reshape(128, 128).astype(BF16)
    for copy in sent:
        copy.wait_send()


def body(sizes, activations, out_grad, weight):
    ny, nz, nx, nf = sizes
    nc = nx * 2
    own_filt = out_grad.shape[1]
    cells = 16 * 128 * ny * nz
    dma = pltpu.SemaphoreType.DMA
    vmem = pl.BlockSpec(memory_space=pltpu.VMEM)
    hbm = pl.BlockSpec(memory_space=pl.ANY)
    y_rows = ROWS // ny
    z_rows = y_rows // nz
    pairs = []
    for shape in (
        (nc - 1,), (2,), (nf - 1,), (nf - 1,), (ny - 1,), (nf - 1, max(nx - 1, 1)), (nf - 1, nx),
        (ny - 1,), (nz - 1,), (nz - 1,), (ny - 1,), (2,),
    ):
        pairs += [dma(shape), dma(shape)]
    gi, gw = pl.pallas_call(
        functools.partial(kernel, sizes, 1.0 / math.sqrt(cells)),
        out_shape=(
            jax.ShapeDtypeStruct((128, 128), BF16),
            jax.ShapeDtypeStruct((27, 32, 64), F32),
        ),
        in_specs=[hbm] * 3,
        out_specs=(vmem, vmem),
        scratch_shapes=[
            pltpu.VMEM(activations.shape, BF16),
            pltpu.VMEM(out_grad.shape, BF16),
            pltpu.VMEM(weight.shape, BF16),
            pltpu.VMEM((4, 4, 32, 128), F32),
            pltpu.VMEM((4, 4, own_filt, 128), F32),
            pltpu.VMEM((16 * own_filt, 128), BF16),
            pltpu.VMEM((nf, TAP_ROWS, 128), BF16),
            dma((3,)),
            pltpu.SemaphoreType.REGULAR((nf - 1,)),
            pltpu.VMEM((nf, nc, 16 * own_filt, 128), BF16),
            pltpu.VMEM((6, 6, 32, 128), BF16),
            pltpu.VMEM((ny, nf - 1, TAP_ROWS // ny, 128), BF16),
            pltpu.VMEM((256, 256), BF16),
            pltpu.VMEM((288, 256), F32),
            pltpu.VMEM((ROWS, 128), F32),
            pltpu.VMEM((ny - 1, y_rows, 128), F32),
            pltpu.VMEM((y_rows, 128), F32),
            pltpu.VMEM((nz - 1, z_rows, 128), F32),
            pltpu.VMEM((ROWS, 128), F32),
            pltpu.VMEM((8, 6, 256, 128), F32),
            pltpu.VMEM((6, 4, 8, 128), F32),
            pltpu.VMEM((2, 4, 8, 128), F32),
        ] + pairs,
        compiler_params=pltpu.CompilerParams(
            collective_id=0, has_side_effects=True, vmem_limit_bytes=32 * 1024 * 1024
        ),
    )(activations, out_grad, weight)
    return jnp.transpose(gi.reshape(4, 4, 8, 128), (2, 0, 1, 3)), gw


def solution(mesh):
    ns = mesh.shape["space"]
    nz = 8 if ns % 8 == 0 else 2
    sizes = (ns // nz, nz, mesh.shape["chan"] // 2, mesh.shape["filt"])
    return jax.shard_map(
        functools.partial(body, sizes),
        mesh=mesh,
        in_specs=(
            P("chan", "space", None, None),
            P("filt", "chan", "space", None, None),
            P(None, "chan", "filt"),
        ),
        out_specs=(P(("chan", "filt"), "space", None, None), P(None, "chan", "filt")),
        check_vma=False,
    )
```

```python
import functools
import math

import jax
import jax.numpy as jnp
from jax import lax
from jax.experimental import pallas as pl
from jax.experimental.pallas import tpu as pltpu
from jax.sharding import PartitionSpec as P

MESH = pl.DeviceIdType.MESH
F32, BF16 = jnp.float32, jnp.bfloat16
ROWS = 512
TAP_ROWS = 128


def kernel(
    sizes, scale,
    act_hbm, shard_hbm, weight_hbm,
    gi_ref, gw_ref,
    act_raw, shard_raw, weight_raw, act_stage, shard_stage, shard_ref, taps_ref, in_sems, told,
    grads, acts, wparts, lhs, late, acc, mine, from_y, for_z, from_z, total, prod, outs, halo,
    s_own, r_own, s_act, r_act, s_filt, r_filt, s_wf, r_wf, s_wy, r_wy, s_pass, r_pass, s_edge, r_edge, s_pe, r_pe,
    s_yr, r_yr, s_zr, r_zr, s_zg, r_zg, s_yg, r_yg, s_halo, r_halo,
):
    ny, nz, nx, nf = sizes
    nc, ns = nx * 2, ny * nz
    space, chan, filt = lax.axis_index("space"), lax.axis_index("chan"), lax.axis_index("filt")
    row, run = space // nz, space % nz
    chip, core = chan // 2, chan % 2
    shard_rows = shard_ref.shape[0]
    own_filt = shard_rows // 16
    y_rows = ROWS // ny
    z_rows = y_rows // nz
    w_rows = TAP_ROWS // (2 * ny)
    layer_rows = 4 * own_filt
    inner_rows = pl.ds(layer_rows, 4 * layer_rows)
    w_mine = row * 2 + run % 2
    before, after = (space + ns - 1) % ns, (space + 1) % ns
    at_low, at_high = run == 0, run == nz - 1
    at_end = jnp.logical_or(at_low, at_high)
    across = jnp.where(at_low, before, after)
    edge_from = jnp.where(at_low, 0, 3)
    edge_to = jnp.where(at_low, 5, 0)
    edge_in = jnp.where(at_low, 0, 5)

    def layers(x):
        return pl.ds(pl.multiple_of(x * layer_rows, layer_rows), layer_rows)

    def at_y(d):
        return {"space": ((row + d) % ny) * nz + run}

    def at_z(d):
        return {"space": row * nz + (run + d) % nz}

    def at_w(e):
        return {"space": (row + e // 2) % ny * nz + (run + e % 2 - 2 * (e % 2) * (run % 2))}


    def filt_at(d):
        return (filt + d) % nf

    barrier = pltpu.get_barrier_semaphore()
    partners = [{"chan": (chan + d) % nc} for d in range(1, nc)]
    partners += [at_y(d) for d in range(1, ny)] + [at_z(d) for d in range(1, nz)]
    partners += [{"space": before}, {"space": after}]
    partners += [at_w(2 * e + 1) for e in range(1, ny)]
    for partner in partners:
        pl.semaphore_signal(barrier, inc=1, device_id=partner, device_id_type=MESH)
    for d in range(1, nf):
        target = filt_at(d)

        @pl.when(filt < target)
        def _(target=target):
            pl.semaphore_signal(barrier, inc=1, device_id={"filt": target}, device_id_type=MESH)

            @pl.when(at_end)
            def _():
                where = {"filt": target, "space": across}
                pl.semaphore_signal(barrier, inc=1, device_id=where, device_id_type=MESH)

    loads = [
        pltpu.make_async_copy(src, dst, in_sems.at[n])
        for n, (src, dst) in enumerate(((shard_hbm, shard_raw), (act_hbm, act_raw), (weight_hbm, weight_raw)))
    ]
    for load in loads:
        load.start()

    sent = []

    def remote(src, dst, ssem, rsem, where, start=True, log=True):
        copy = pltpu.make_async_remote_copy(
            src_ref=src, dst_ref=dst, send_sem=ssem, recv_sem=rsem, device_id=where, device_id_type=MESH
        )
        if start:
            copy.start()
        if log:
            sent.append(copy)
        return copy

    lane = lax.broadcasted_iota(jnp.int32, (1, 128), 1)
    first, last = lane == 0, lane == 127
    loads[0].wait()
    for o in range(own_filt):
        shard_stage[:, :, o, :] = shard_raw[0, o].astype(F32)
    shard_ref[...] = shard_stage[...].reshape(shard_rows, 128).astype(BF16)
    grads[0, chan, inner_rows] = shard_ref[...]
    loads[1].wait()
    for i in range(32):
        act_stage[:, :, i, :] = act_raw[i].astype(F32)
    acts[1:5, 1:5] = act_stage[...].astype(BF16)
    empty = jnp.zeros((6, 32, 128), BF16)
    acts[:, 0] = empty
    acts[:, 5] = empty
    loads[2].wait()
    blank = jnp.zeros((8, 64), F32)
    for block in range(nf):
        pieces = []
        for k in range(0, 32, 2):
            pair = [
                weight_raw[t].astype(F32)[block * 8 : block * 8 + 8] if t < 27 else blank for t in (k, k + 1)
            ]
            pieces.append(jnp.concatenate(pair, axis=1))
        taps_ref[block] = jnp.concatenate(pieces, axis=0).astype(BF16)
    acc[...] = jnp.zeros(acc.shape, F32)
    pl.semaphore_wait(barrier, len(partners) + filt * jnp.where(at_end, 2, 1))

    over, wover, edge = {}, {}, {}
    for d in range(nf):
        target = filt_at(d)
        edge[d] = remote(
            shard_ref.at[layers(edge_from)], grads.at[d, chan, layers(edge_to)],
            s_edge.at[d], r_edge.at[d], {"filt": target, "space": across}, start=False, log=False,
        )
        if d > 0:
            over[d] = remote(
                shard_ref, grads.at[d, chan, inner_rows], s_filt.at[d - 1], r_filt.at[d - 1],
                {"filt": target}, start=False,
            )
            wover[d] = remote(
                taps_ref.at[target, pl.ds(pl.multiple_of(w_mine * w_rows, w_rows), w_rows)],
                wparts.at[w_mine, d - 1], s_wf.at[d - 1], r_wf.at[d - 1], {"filt": target}, start=False,
            )

    def send_over(d):
        wover[d].start()
        over[d].start()
        pl.when(at_end)(edge[d].start)

    def tell(d):
        target = filt_at(d)

        @pl.when(filt > target)
        def _():
            pl.semaphore_signal(told.at[d - 1, 0], inc=1, device_id={"filt": target}, device_id_type=MESH)

            @pl.when(at_end)
            def _():
                where = {"filt": target, "space": across}
                pl.semaphore_signal(told.at[d - 1, 1], inc=1, device_id=where, device_id_type=MESH)

    def send_back(d, who):
        pl.when(filt == who)(lambda: send_over(d))

    def send_on(d, who):
        @pl.when(functools.reduce(jnp.logical_or, [filt == w for w in who]))
        def _():
            pl.semaphore_wait(told.at[nf - d - 1, 0], 1)

            @pl.when(at_end)
            def _():
                pl.semaphore_wait(told.at[nf - d - 1, 1], 1)

            send_over(d)

    for d in (2, 1, 3):
        tell(d)
    for d in range(1, nf):
        send_back(d, nf - d)
    pl.when(at_end)(edge[0].start)
    own = [
        remote(
            shard_ref, grads.at[0, chan, inner_rows], s_own.at[d - 1], r_own.at[d - 1], {"chan": (chan + d) % nc}
        )
        for d in range(1, nc)
    ]
    up = remote(acts.at[4, pl.ds(1, 4)], acts.at[0, pl.ds(1, 4)], s_act.at[0], r_act.at[0], {"space": after})
    down = remote(acts.at[1, pl.ds(1, 4)], acts.at[5, pl.ds(1, 4)], s_act.at[1], r_act.at[1], {"space": before})

    rim = jnp.zeros((6, 256, 128), F32)
    for x in (0, 1, 6, 7):
        prod[x] = rim
    for x in range(2, 6):
        prod[x, 0] = rim[0]
        prod[x, 5] = rim[0]

    for copy in own:
        copy.wait_recv()
    up.wait_recv()
    down.wait_recv()
    zero = jnp.zeros((4, 32, 128), BF16)
    acts[0, 1:5] = jnp.where(space > 0, acts[0, 1:5], zero)
    acts[5, 1:5] = jnp.where(space < ns - 1, acts[5, 1:5], zero)

    def pair_of(block):
        parts = block.astype(F32).reshape(-1, 2, own_filt, 128)
        return [parts[:, i].reshape(-1, 128) for i in range(2)]

    def taps_step(h, carry):
        x, z = h // 2, (h % 2) * 2
        start = pl.multiple_of(h * 2 * own_filt, 2 * own_filt)
        columns = []
        for g in pair_of(grads[0, :, pl.ds(start + layer_rows, 2 * own_filt), :]):
            low = jnp.where(last, 0.0, pltpu.roll(g, 127, 1))
            high = jnp.where(first, 0.0, pltpu.roll(g, 1, 1))
            columns.append(jnp.concatenate([low, g, high], axis=0).astype(BF16))
        rhs = jnp.concatenate(columns, axis=1)
        halves = [
            jnp.concatenate([acts[x + a, z + c + i] for a in range(3) for c in range(3)], axis=0)
            for i in range(2)
        ]
        acc[:, 0:192] += lax.dot_general(
            jnp.concatenate(halves, axis=1), rhs, (((1,), (1,)), ((), ())), preferred_element_type=F32
        )
        return carry

    lax.fori_loop(0, 8, taps_step, 0)
    mine[0:288] = acc[:, 0:128] * scale
    third = acc[:, 128:256] * scale
    mine[288:432] = jnp.where(lane < 64, third[0:144], pltpu.roll(third[144:288], 64, 1))
    mine[432:512] = jnp.zeros((80, 128), F32)

    y_red = []
    for d in range(1, ny):
        theirs = pl.multiple_of((row + d) % ny * y_rows, y_rows)
        y_red.append(
            remote(mine.at[pl.ds(theirs, y_rows)], from_y.at[d - 1], s_yr.at[d - 1], r_yr.at[d - 1], at_y(d))
        )

    passed, passed_edge = {}, {}

    def pass_edge(d):
        for e in range(1, nc):
            block = grads.at[d, chan, layers(edge_in)]
            passed_edge[d, e] = remote(
                block, block, s_pe.at[d, e - 1], r_pe.at[d, e - 1], {"chan": (chan + e) % nc}, start=False, log=False
            )

        @pl.when(at_end)
        def _():
            edge[d].wait_recv()
            for e in range(1, nc):
                passed_edge[d, e].start()

    def forward(d):
        over[d].wait_recv()
        for e in range(1, nc):
            block = grads.at[d, chan, inner_rows]
            passed[d, e] = remote(
                block, block, s_pass.at[d - 1, e - 1], r_pass.at[d - 1, e - 1], {"chan": (chan + e) % nc}
            )
        pass_edge(d)

    def take(which):
        for (d, e), copy in passed.items():
            if d in which:
                copy.wait_recv()

        @pl.when(at_end)
        def _():
            for (d, e), copy in passed_edge.items():
                if d in which:
                    copy.wait_recv()

    for d, who in ((3, 2), (2, 3), (3, 3)):
        send_back(d, who)
    send_on(1, (1, 2))
    send_on(2, (1,))
    pass_edge(0)

    mine_y = pl.multiple_of(row * y_rows, y_rows)
    for copy in y_red:
        copy.wait_recv()
    part = mine[pl.ds(mine_y, y_rows)]
    for d in range(1, ny):
        part = part + from_y[d - 1]
    for_z[...] = part
    z_red = []
    for d in range(1, nz):
        theirs = pl.multiple_of((run + d) % nz * z_rows, z_rows)
        z_red.append(
            remote(for_z.at[pl.ds(theirs, z_rows)], from_z.at[d - 1], s_zr.at[d - 1], r_zr.at[d - 1], at_z(d))
        )

    send_on(1, (0,))
    send_on(3, (0,))
    wshare = {}

    def share_weights(d):
        wover[d].wait_recv()
        block = wparts.at[w_mine, d - 1]
        for e in range(1, 2 * ny):
            wshare[d, e] = remote(block, block, s_wy.at[d - 1, e - 1], r_wy.at[d - 1, e - 1], at_w(e))

    def widen(out, column, a, b):
        a = a.astype(F32)
        b = jnp.zeros_like(a) if b is None else b.astype(F32)
        columns = slice(column, column + 128)
        out[0:128, columns] = jnp.where(lane < 64, a, pltpu.roll(b, 64, 1)).astype(BF16)
        out[128:256, columns] = jnp.where(lane < 64, pltpu.roll(a, 64, 1), b).astype(BF16)

    forward(1)
    forward(3)

    for copy in z_red:
        copy.wait_recv()
    part = for_z[pl.ds(pl.multiple_of(run * z_rows, z_rows), z_rows)]
    for d in range(1, nz):
        part = part + from_z[d - 1]
    place = pl.ds(pl.multiple_of(mine_y + run * z_rows, z_rows), z_rows)
    total[place] = part
    z_gat = [
        remote(total.at[place], total.at[place], s_zg.at[d - 1], r_zg.at[d - 1], at_z(d)) for d in range(1, nz)
    ]
    send_on(2, (0,))
    share_weights(1)
    share_weights(3)
    forward(2)
    share_weights(2)
    for (d, e), copy in wshare.items():
        if d != 2:
            copy.wait_recv()
    widen(lhs, 0, taps_ref[filt], wparts[:, 0].reshape(TAP_ROWS, 128))
    widen(lhs, 128, wparts[:, 2].reshape(TAP_ROWS, 128), None)
    lowest = jnp.where(jnp.logical_and(at_low, space > 0), 0, 2)
    highest = jnp.where(jnp.logical_and(at_high, space < ns - 1), 12, 10)

    def product(which, left, add):
        def step(h, carry):
            x, z = h // 2, (h % 2) * 2
            start = pl.multiple_of(h * 2 * own_filt, 2 * own_filt)
            parts = [pair_of(grads[d, :, pl.ds(start, 2 * own_filt), :]) for d in which]
            rhs = jnp.concatenate(
                [jnp.concatenate([p[i] for p in parts], axis=0) for i in range(2)], axis=1
            ).astype(BF16)
            result = jnp.dot(left[:, 0 : 64 * len(which)], rhs, preferred_element_type=F32)
            for i in range(2):
                half = result[:, i * 128 : i * 128 + 128]
                prod[x + 1, z + 1 + i] = prod[x + 1, z + 1 + i] + half if add else half
            return carry

        lax.fori_loop(lowest, highest, step, 0)

    take((0, 1, 3))
    product((0, 1, 3), lhs, False)
    for copy in z_gat:
        copy.wait_recv()
    place_y = pl.ds(mine_y, y_rows)
    y_gat = [
        remote(total.at[place_y], total.at[place_y], s_yg.at[d - 1], r_yg.at[d - 1], at_y(d)) for d in range(1, ny)
    ]

    for (d, e), copy in wshare.items():
        if d == 2:
            copy.wait_recv()
    widen(late, 0, wparts[:, 1].reshape(TAP_ROWS, 128), None)
    take((2,))
    product((2,), late, True)

    def sum_step(n, x):
        z = n
        sums = []
        for b in range(3):
            terms = []
            for a in range(3):
                for c in range(3):
                    k = (a * 3 + b) * 3 + c
                    at = (k % 2) * 128 + (k // 2) * 8
                    terms.append(prod[x + 2 - a, z + 2 - c, at : at + 8])
            sums.append(functools.reduce(jnp.add, terms))
        low = jnp.where(last, 0.0, pltpu.roll(sums[0], 127, 1))
        high = jnp.where(first, 0.0, pltpu.roll(sums[2], 1, 1))
        outs[x, z] = sums[1] + low + high
        return x

    def layer(x):
        for n in range(4):
            sum_step(n, x)

    low_out = remote(
        outs.at[0], halo.at[1], s_halo.at[0], r_halo.at[0], {"space": before}, start=False, log=False
    )
    high_out = remote(
        outs.at[5], halo.at[0], s_halo.at[1], r_halo.at[1], {"space": after}, start=False, log=False
    )

    @pl.when(jnp.logical_not(at_low))
    def _():
        layer(0)
        low_out.start()

    @pl.when(jnp.logical_not(at_high))
    def _():
        layer(5)
        high_out.start()

    def inner(x, carry):
        layer(x)
        return carry

    lax.fori_loop(1, 5, inner, 0)

    for copy in y_gat:
        copy.wait_recv()
    for a in range(3):
        for c in range(3):
            block = (a * 3 + c) * 32
            for b in range(2):
                gw_ref[(a * 3 + b) * 3 + c] = total[block : block + 32, b * 64 : b * 64 + 64]
            for half in range(2):
                at = block + half * 16
                left = 0 if at < 144 else 64
                src = 288 + (at if at < 144 else at - 144)
                gw_ref[(a * 3 + 2) * 3 + c, half * 16 : half * 16 + 16] = total[src : src + 16, left : left + 64]

    @pl.when(jnp.logical_not(at_low))
    def _():
        high_out.wait_recv()
        outs[1] = outs[1] + halo[0]
        low_out.wait_send()

    @pl.when(jnp.logical_not(at_high))
    def _():
        low_out.wait_recv()
        outs[4] = outs[4] + halo[1]
        high_out.wait_send()

    gi_ref[...] = outs[1:5].reshape(128, 128).astype(BF16)
    for copy in sent:
        copy.wait_send()

    @pl.when(at_end)
    def _():
        for copy in list(edge.values()) + list(passed_edge.values()):
            copy.wait_send()


def body(sizes, activations, out_grad, weight):
    ny, nz, nx, nf = sizes
    nc = nx * 2
    own_filt = out_grad.shape[1]
    cells = 16 * 128 * ny * nz
    dma = pltpu.SemaphoreType.DMA
    vmem = pl.BlockSpec(memory_space=pltpu.VMEM)
    hbm = pl.BlockSpec(memory_space=pl.ANY)
    y_rows = ROWS // ny
    z_rows = y_rows // nz
    pairs = []
    for shape in (
        (nc - 1,), (2,), (nf - 1,), (nf - 1,), (nf - 1, 2 * ny - 1), (nf - 1, nc - 1), (nf,), (nf, nc - 1),
        (ny - 1,), (nz - 1,), (nz - 1,), (ny - 1,), (2,),
    ):
        pairs += [dma(shape), dma(shape)]
    gi, gw = pl.pallas_call(
        functools.partial(kernel, sizes, 1.0 / math.sqrt(cells)),
        out_shape=(
            jax.ShapeDtypeStruct((128, 128), BF16),
            jax.ShapeDtypeStruct((27, 32, 64), F32),
        ),
        in_specs=[hbm] * 3,
        out_specs=(vmem, vmem),
        scratch_shapes=[
            pltpu.VMEM(activations.shape, BF16),
            pltpu.VMEM(out_grad.shape, BF16),
            pltpu.VMEM(weight.shape, BF16),
            pltpu.VMEM((4, 4, 32, 128), F32),
            pltpu.VMEM((4, 4, own_filt, 128), F32),
            pltpu.VMEM((16 * own_filt, 128), BF16),
            pltpu.VMEM((nf, TAP_ROWS, 128), BF16),
            dma((3,)),
            pltpu.SemaphoreType.REGULAR((nf - 1, 2)),
            pltpu.VMEM((nf, nc, 24 * own_filt, 128), BF16),
            pltpu.VMEM((6, 6, 32, 128), BF16),
            pltpu.VMEM((2 * ny, nf - 1, TAP_ROWS // (2 * ny), 128), BF16),
            pltpu.VMEM((256, 256), BF16),
            pltpu.VMEM((256, 128), BF16),
            pltpu.VMEM((288, 256), F32),
            pltpu.VMEM((ROWS, 128), F32),
            pltpu.VMEM((ny - 1, y_rows, 128), F32),
            pltpu.VMEM((y_rows, 128), F32),
            pltpu.VMEM((nz - 1, z_rows, 128), F32),
            pltpu.VMEM((ROWS, 128), F32),
            pltpu.VMEM((8, 6, 256, 128), F32),
            pltpu.VMEM((6, 4, 8, 128), F32),
            pltpu.VMEM((2, 4, 8, 128), F32),
        ] + pairs,
        compiler_params=pltpu.CompilerParams(
            collective_id=0, has_side_effects=True, vmem_limit_bytes=63 * 1024 * 1024
        ),
    )(activations, out_grad, weight)
    return jnp.transpose(gi.reshape(4, 4, 8, 128), (2, 0, 1, 3)), gw


def solution(mesh):
    ns = mesh.shape["space"]
    nz = 8 if ns % 8 == 0 else 2
    sizes = (ns // nz, nz, mesh.shape["chan"] // 2, mesh.shape["filt"])
    return jax.shard_map(
        functools.partial(body, sizes),
        mesh=mesh,
        in_specs=(
            P("chan", "space", None, None),
            P("filt", "chan", "space", None, None),
            P(None, "chan", "filt"),
        ),
        out_specs=(P(("chan", "filt"), "space", None, None), P(None, "chan", "filt")),
        check_vma=False,
    )
```

```python
import functools
import math

import jax
import jax.numpy as jnp
from jax import lax
from jax.experimental import pallas as pl
from jax.experimental.pallas import tpu as pltpu
from jax.sharding import PartitionSpec as P

MESH = pl.DeviceIdType.MESH
F32, BF16 = jnp.float32, jnp.bfloat16
ROWS = 512
TAP_ROWS = 128


def kernel(
    sizes, scale,
    act_hbm, shard_hbm, weight_hbm,
    gi_ref, gw_ref,
    act_raw, shard_raw, weight_raw, act_stage, shard_stage, shard_ref, taps_ref, in_sems, told,
    grads, acts, wparts, lhs, late, acc, mine, from_y, for_z, from_z, total, prod, outs, halo,
    s_own, r_own, s_act, r_act, s_filt, r_filt, s_wf, r_wf, s_wy, r_wy, s_pass, r_pass, s_edge, r_edge, s_pe, r_pe,
    s_yr, r_yr, s_zr, r_zr, s_zg, r_zg, s_yg, r_yg, s_halo, r_halo,
):
    ny, nz, nx, nf = sizes
    nc, ns = nx * 2, ny * nz
    space, chan, filt = lax.axis_index("space"), lax.axis_index("chan"), lax.axis_index("filt")
    row, run = space // nz, space % nz
    chip, core = chan // 2, chan % 2
    shard_rows = shard_ref.shape[0]
    own_filt = shard_rows // 16
    y_rows = ROWS // ny
    z_rows = y_rows // nz
    w_rows = TAP_ROWS // (2 * ny)
    layer_rows = 4 * own_filt
    inner_rows = pl.ds(layer_rows, 4 * layer_rows)
    w_mine = row * 2 + run % 2
    before, after = (space + ns - 1) % ns, (space + 1) % ns
    at_low, at_high = run == 0, run == nz - 1
    at_end = jnp.logical_or(at_low, at_high)
    across = jnp.where(at_low, before, after)
    edge_from = jnp.where(at_low, 0, 3)
    edge_to = jnp.where(at_low, 5, 0)
    edge_in = jnp.where(at_low, 0, 5)

    def layers(x):
        return pl.ds(pl.multiple_of(x * layer_rows, layer_rows), layer_rows)

    def at_y(d):
        return {"space": ((row + d) % ny) * nz + run}

    def at_z(d):
        return {"space": row * nz + (run + d) % nz}

    def at_w(e):
        return {"space": (row + e // 2) % ny * nz + (run + e % 2 - 2 * (e % 2) * (run % 2))}


    def filt_at(d):
        return (filt + d) % nf

    barrier = pltpu.get_barrier_semaphore()
    partners = [{"chan": (chan + d) % nc} for d in range(1, nc)]
    partners += [at_y(d) for d in range(1, ny)] + [at_z(d) for d in range(1, nz)]
    partners += [{"space": before}, {"space": after}]
    partners += [at_w(2 * e + 1) for e in range(1, ny)]
    for partner in partners:
        pl.semaphore_signal(barrier, inc=1, device_id=partner, device_id_type=MESH)
    for d in range(1, nf):
        target = filt_at(d)

        @pl.when(filt < target)
        def _(target=target):
            pl.semaphore_signal(barrier, inc=1, device_id={"filt": target}, device_id_type=MESH)

            @pl.when(at_end)
            def _():
                where = {"filt": target, "space": across}
                pl.semaphore_signal(barrier, inc=1, device_id=where, device_id_type=MESH)

    loads = [
        pltpu.make_async_copy(src, dst, in_sems.at[n])
        for n, (src, dst) in enumerate(((shard_hbm, shard_raw), (act_hbm, act_raw), (weight_hbm, weight_raw)))
    ]
    for load in loads:
        load.start()

    sent = []

    def remote(src, dst, ssem, rsem, where, start=True, log=True):
        copy = pltpu.make_async_remote_copy(
            src_ref=src, dst_ref=dst, send_sem=ssem, recv_sem=rsem, device_id=where, device_id_type=MESH
        )
        if start:
            copy.start()
        if log:
            sent.append(copy)
        return copy

    lane = lax.broadcasted_iota(jnp.int32, (1, 128), 1)
    first, last = lane == 0, lane == 127
    loads[0].wait()
    for o in range(own_filt):
        shard_stage[:, :, o, :] = shard_raw[0, o].astype(F32)
    shard_ref[...] = shard_stage[...].reshape(shard_rows, 128).astype(BF16)
    grads[0, chan, inner_rows] = shard_ref[...]
    loads[1].wait()
    for i in range(32):
        act_stage[:, :, i, :] = act_raw[i].astype(F32)
    acts[1:5, 1:5] = act_stage[...].astype(BF16)
    empty = jnp.zeros((6, 32, 128), BF16)
    acts[:, 0] = empty
    acts[:, 5] = empty
    loads[2].wait()
    blank = jnp.zeros((8, 64), F32)
    for block in range(nf):
        pieces = []
        for k in range(0, 32, 2):
            pair = [
                weight_raw[t].astype(F32)[block * 8 : block * 8 + 8] if t < 27 else blank for t in (k, k + 1)
            ]
            pieces.append(jnp.concatenate(pair, axis=1))
        taps_ref[block] = jnp.concatenate(pieces, axis=0).astype(BF16)
    acc[...] = jnp.zeros(acc.shape, F32)
    pl.semaphore_wait(barrier, len(partners) + filt * jnp.where(at_end, 2, 1))

    over, wover, edge = {}, {}, {}
    for d in range(nf):
        target = filt_at(d)
        edge[d] = remote(
            shard_ref.at[layers(edge_from)], grads.at[d, chan, layers(edge_to)],
            s_edge.at[d], r_edge.at[d], {"filt": target, "space": across}, start=False, log=False,
        )
        if d > 0:
            over[d] = remote(
                shard_ref, grads.at[d, chan, inner_rows], s_filt.at[d - 1], r_filt.at[d - 1],
                {"filt": target}, start=False,
            )
            wover[d] = remote(
                taps_ref.at[target, pl.ds(pl.multiple_of(w_mine * w_rows, w_rows), w_rows)],
                wparts.at[w_mine, d - 1], s_wf.at[d - 1], r_wf.at[d - 1], {"filt": target}, start=False,
            )

    def send_over(d):
        wover[d].start()
        over[d].start()
        pl.when(at_end)(lambda: edge[d].start())

    def tell(d):
        target = filt_at(d)

        @pl.when(filt > target)
        def _():
            pl.semaphore_signal(told.at[d - 1, 0], inc=1, device_id={"filt": target}, device_id_type=MESH)

            @pl.when(at_end)
            def _():
                where = {"filt": target, "space": across}
                pl.semaphore_signal(told.at[d - 1, 1], inc=1, device_id=where, device_id_type=MESH)

    def send_back(d, who):
        pl.when(filt == who)(lambda: send_over(d))

    def send_on(d, who):
        @pl.when(functools.reduce(jnp.logical_or, [filt == w for w in who]))
        def _():
            pl.semaphore_wait(told.at[nf - d - 1, 0], 1)

            @pl.when(at_end)
            def _():
                pl.semaphore_wait(told.at[nf - d - 1, 1], 1)

            send_over(d)

    for d in (2, 1, 3):
        tell(d)
    for d in range(1, nf):
        send_back(d, nf - d)
    pl.when(at_end)(edge[0].start)
    own = [
        remote(
            shard_ref, grads.at[0, chan, inner_rows], s_own.at[d - 1], r_own.at[d - 1], {"chan": (chan + d) % nc}
        )
        for d in range(1, nc)
    ]
    up = remote(acts.at[4, pl.ds(1, 4)], acts.at[0, pl.ds(1, 4)], s_act.at[0], r_act.at[0], {"space": after})
    down = remote(acts.at[1, pl.ds(1, 4)], acts.at[5, pl.ds(1, 4)], s_act.at[1], r_act.at[1], {"space": before})

    rim = jnp.zeros((6, 256, 128), F32)
    for x in (0, 1, 6, 7):
        prod[x] = rim
    for x in range(2, 6):
        prod[x, 0] = rim[0]
        prod[x, 5] = rim[0]

    for copy in own:
        copy.wait_recv()
    up.wait_recv()
    down.wait_recv()
    zero = jnp.zeros((4, 32, 128), BF16)
    acts[0, 1:5] = jnp.where(space > 0, acts[0, 1:5], zero)
    acts[5, 1:5] = jnp.where(space < ns - 1, acts[5, 1:5], zero)

    def pair_of(block):
        parts = block.astype(F32).reshape(-1, 2, own_filt, 128)
        return [parts[:, i].reshape(-1, 128) for i in range(2)]

    def taps_step(h, carry):
        x, z = h // 2, (h % 2) * 2
        start = pl.multiple_of(h * 2 * own_filt, 2 * own_filt)
        columns = []
        for g in pair_of(grads[0, :, pl.ds(start + layer_rows, 2 * own_filt), :]):
            low = jnp.where(last, 0.0, pltpu.roll(g, 127, 1))
            high = jnp.where(first, 0.0, pltpu.roll(g, 1, 1))
            columns.append(jnp.concatenate([low, g, high], axis=0).astype(BF16))
        rhs = jnp.concatenate(columns, axis=1)
        halves = [
            jnp.concatenate([acts[x + a, z + c + i] for a in range(3) for c in range(3)], axis=0)
            for i in range(2)
        ]
        acc[:, 0:192] += lax.dot_general(
            jnp.concatenate(halves, axis=1), rhs, (((1,), (1,)), ((), ())), preferred_element_type=F32
        )
        return carry

    lax.fori_loop(0, 8, taps_step, 0)
    mine[0:288] = acc[:, 0:128] * scale
    third = acc[:, 128:256] * scale
    mine[288:432] = jnp.where(lane < 64, third[0:144], pltpu.roll(third[144:288], 64, 1))
    mine[432:512] = jnp.zeros((80, 128), F32)

    y_red = []
    for d in range(1, ny):
        theirs = pl.multiple_of((row + d) % ny * y_rows, y_rows)
        y_red.append(
            remote(mine.at[pl.ds(theirs, y_rows)], from_y.at[d - 1], s_yr.at[d - 1], r_yr.at[d - 1], at_y(d))
        )

    passed, passed_edge = {}, {}

    def pass_edge(d):
        for e in range(1, nc):
            block = grads.at[d, chan, layers(edge_in)]
            passed_edge[d, e] = remote(
                block, block, s_pe.at[d, e - 1], r_pe.at[d, e - 1], {"chan": (chan + e) % nc}, start=False, log=False
            )

        @pl.when(at_end)
        def _():
            edge[d].wait_recv()
            for e in range(1, nc):
                passed_edge[d, e].start()

    def forward(d):
        over[d].wait_recv()
        for e in range(1, nc):
            block = grads.at[d, chan, inner_rows]
            passed[d, e] = remote(
                block, block, s_pass.at[d - 1, e - 1], r_pass.at[d - 1, e - 1], {"chan": (chan + e) % nc}
            )
        pass_edge(d)

    def take(which):
        for (d, e), copy in passed.items():
            if d in which:
                copy.wait_recv()

        @pl.when(at_end)
        def _():
            for (d, e), copy in passed_edge.items():
                if d in which:
                    copy.wait_recv()

    for d, who in ((3, 2), (2, 3), (3, 3)):
        send_back(d, who)
    send_on(1, (1, 2))
    send_on(2, (1,))
    pass_edge(0)

    mine_y = pl.multiple_of(row * y_rows, y_rows)
    for copy in y_red:
        copy.wait_recv()
    part = mine[pl.ds(mine_y, y_rows)]
    for d in range(1, ny):
        part = part + from_y[d - 1]
    for_z[...] = part
    z_red = []
    for d in range(1, nz):
        theirs = pl.multiple_of((run + d) % nz * z_rows, z_rows)
        z_red.append(
            remote(for_z.at[pl.ds(theirs, z_rows)], from_z.at[d - 1], s_zr.at[d - 1], r_zr.at[d - 1], at_z(d))
        )

    send_on(1, (0,))
    send_on(3, (0,))
    wshare = {}

    def share_weights(d):
        wover[d].wait_recv()
        block = wparts.at[w_mine, d - 1]
        for e in range(1, 2 * ny):
            wshare[d, e] = remote(block, block, s_wy.at[d - 1, e - 1], r_wy.at[d - 1, e - 1], at_w(e))

    def widen(out, column, a, b):
        a = a.astype(F32)
        b = jnp.zeros_like(a) if b is None else b.astype(F32)
        columns = slice(column, column + 128)
        out[0:128, columns] = jnp.where(lane < 64, a, pltpu.roll(b, 64, 1)).astype(BF16)
        out[128:256, columns] = jnp.where(lane < 64, pltpu.roll(a, 64, 1), b).astype(BF16)

    forward(1)
    forward(3)

    for copy in z_red:
        copy.wait_recv()
    part = for_z[pl.ds(pl.multiple_of(run * z_rows, z_rows), z_rows)]
    for d in range(1, nz):
        part = part + from_z[d - 1]
    place = pl.ds(pl.multiple_of(mine_y + run * z_rows, z_rows), z_rows)
    total[place] = part
    z_gat = [
        remote(total.at[place], total.at[place], s_zg.at[d - 1], r_zg.at[d - 1], at_z(d)) for d in range(1, nz)
    ]
    send_on(2, (0,))
    share_weights(1)
    share_weights(3)
    share_weights(2)
    forward(2)
    for copy in z_gat:
        copy.wait_recv()
    place_y = pl.ds(mine_y, y_rows)
    y_gat = [
        remote(total.at[place_y], total.at[place_y], s_yg.at[d - 1], r_yg.at[d - 1], at_y(d)) for d in range(1, ny)
    ]

    for (d, e), copy in wshare.items():
        if d != 2:
            copy.wait_recv()
    widen(lhs, 0, taps_ref[filt], wparts[:, 0].reshape(TAP_ROWS, 128))
    widen(lhs, 128, wparts[:, 2].reshape(TAP_ROWS, 128), None)
    lowest = jnp.where(jnp.logical_and(at_low, space > 0), 0, 2)
    highest = jnp.where(jnp.logical_and(at_high, space < ns - 1), 12, 10)

    def product(which, left, add, steps):
        def step(h, carry):
            x, z = h // 2, (h % 2) * 2
            start = pl.multiple_of(h * 2 * own_filt, 2 * own_filt)
            parts = [pair_of(grads[d, :, pl.ds(start, 2 * own_filt), :]) for d in which]
            rhs = jnp.concatenate(
                [jnp.concatenate([p[i] for p in parts], axis=0) for i in range(2)], axis=1
            ).astype(BF16)
            result = jnp.dot(left[:, 0 : 64 * len(which)], rhs, preferred_element_type=F32)
            for i in range(2):
                half = result[:, i * 128 : i * 128 + 128]
                prod[x + 1, z + 1 + i] = prod[x + 1, z + 1 + i] + half if add else half
            return carry

        lax.fori_loop(*steps, step, 0)

    take((0, 1, 3))
    product((0, 1, 3), lhs, False, (lowest, highest))
    for (d, e), copy in wshare.items():
        if d == 2:
            copy.wait_recv()
    widen(late, 0, wparts[:, 1].reshape(TAP_ROWS, 128), None)
    take((2,))
    product((2,), late, True, (2, 4))
    product((2,), late, True, (8, 10))

    def sum_step(n, x):
        z = n
        sums = []
        for b in range(3):
            terms = []
            for a in range(3):
                for c in range(3):
                    k = (a * 3 + b) * 3 + c
                    at = (k % 2) * 128 + (k // 2) * 8
                    terms.append(prod[x + 2 - a, z + 2 - c, at : at + 8])
            sums.append(functools.reduce(jnp.add, terms))
        low = jnp.where(last, 0.0, pltpu.roll(sums[0], 127, 1))
        high = jnp.where(first, 0.0, pltpu.roll(sums[2], 1, 1))
        outs[x, z] = sums[1] + low + high
        return x

    def layer(x):
        for n in range(4):
            sum_step(n, x)

    low_out = remote(
        outs.at[0], halo.at[1], s_halo.at[0], r_halo.at[0], {"space": before}, start=False, log=False
    )
    high_out = remote(
        outs.at[5], halo.at[0], s_halo.at[1], r_halo.at[1], {"space": after}, start=False, log=False
    )

    @pl.when(jnp.logical_not(at_low))
    def _():
        layer(0)
        low_out.start()

    @pl.when(jnp.logical_not(at_high))
    def _():
        layer(5)
        high_out.start()

    for steps in ((lowest, 2), (4, 8), (10, highest)):
        product((2,), late, True, steps)

    def inner(x, carry):
        layer(x)
        return carry

    lax.fori_loop(1, 5, inner, 0)

    for copy in y_gat:
        copy.wait_recv()
    for a in range(3):
        for c in range(3):
            block = (a * 3 + c) * 32
            for b in range(2):
                gw_ref[(a * 3 + b) * 3 + c] = total[block : block + 32, b * 64 : b * 64 + 64]
            for half in range(2):
                at = block + half * 16
                left = 0 if at < 144 else 64
                src = 288 + (at if at < 144 else at - 144)
                gw_ref[(a * 3 + 2) * 3 + c, half * 16 : half * 16 + 16] = total[src : src + 16, left : left + 64]

    @pl.when(jnp.logical_not(at_low))
    def _():
        high_out.wait_recv()
        outs[1] = outs[1] + halo[0]
        low_out.wait_send()

    @pl.when(jnp.logical_not(at_high))
    def _():
        low_out.wait_recv()
        outs[4] = outs[4] + halo[1]
        high_out.wait_send()

    for i in range(8):
        gi_ref[i] = outs[1:5, :, i, :].astype(BF16)
    for copy in sent:
        copy.wait_send()

    @pl.when(at_end)
    def _():
        for copy in list(edge.values()) + list(passed_edge.values()):
            copy.wait_send()


def hand_over(gi_in, gw_in, gi_out, gw_out, gi_mid, gw_mid, sems):
    loads = [
        pltpu.make_async_copy(gw_in, gw_mid, sems.at[0]),
        pltpu.make_async_copy(gi_in, gi_mid, sems.at[1]),
    ]
    stores = [
        pltpu.make_async_copy(gw_mid, gw_out, sems.at[2]),
        pltpu.make_async_copy(gi_mid, gi_out, sems.at[3]),
    ]
    for load in loads:
        load.start()
    for load, store in zip(loads, stores):
        load.wait()
        store.start()
    for store in stores:
        store.wait()


def body(sizes, activations, out_grad, weight):
    ny, nz, nx, nf = sizes
    nc = nx * 2
    own_filt = out_grad.shape[1]
    cells = 16 * 128 * ny * nz
    dma = pltpu.SemaphoreType.DMA
    vmem = pl.BlockSpec(memory_space=pltpu.VMEM)
    hbm = pl.BlockSpec(memory_space=pl.ANY)
    y_rows = ROWS // ny
    z_rows = y_rows // nz
    pairs = []
    for shape in (
        (nc - 1,), (2,), (nf - 1,), (nf - 1,), (nf - 1, 2 * ny - 1), (nf - 1, nc - 1), (nf,), (nf, nc - 1),
        (ny - 1,), (nz - 1,), (nz - 1,), (ny - 1,), (2,),
    ):
        pairs += [dma(shape), dma(shape)]
    gi, gw = pl.pallas_call(
        functools.partial(kernel, sizes, 1.0 / math.sqrt(cells)),
        out_shape=(
            jax.ShapeDtypeStruct((8, 4, 4, 128), BF16),
            jax.ShapeDtypeStruct((27, 32, 64), F32),
        ),
        in_specs=[hbm] * 3,
        out_specs=(vmem, vmem),
        scratch_shapes=[
            pltpu.VMEM(activations.shape, BF16),
            pltpu.VMEM(out_grad.shape, BF16),
            pltpu.VMEM(weight.shape, BF16),
            pltpu.VMEM((4, 4, 32, 128), F32),
            pltpu.VMEM((4, 4, own_filt, 128), F32),
            pltpu.VMEM((16 * own_filt, 128), BF16),
            pltpu.VMEM((nf, TAP_ROWS, 128), BF16),
            dma((3,)),
            pltpu.SemaphoreType.REGULAR((nf - 1, 2)),
            pltpu.VMEM((nf, nc, 24 * own_filt, 128), BF16),
            pltpu.VMEM((6, 6, 32, 128), BF16),
            pltpu.VMEM((2 * ny, nf - 1, TAP_ROWS // (2 * ny), 128), BF16),
            pltpu.VMEM((256, 256), BF16),
            pltpu.VMEM((256, 128), BF16),
            pltpu.VMEM((288, 256), F32),
            pltpu.VMEM((ROWS, 128), F32),
            pltpu.VMEM((ny - 1, y_rows, 128), F32),
            pltpu.VMEM((y_rows, 128), F32),
            pltpu.VMEM((nz - 1, z_rows, 128), F32),
            pltpu.VMEM((ROWS, 128), F32),
            pltpu.VMEM((8, 6, 256, 128), F32),
            pltpu.VMEM((6, 4, 8, 128), F32),
            pltpu.VMEM((2, 4, 8, 128), F32),
        ] + pairs,
        compiler_params=pltpu.CompilerParams(
            collective_id=0, has_side_effects=True, vmem_limit_bytes=63 * 1024 * 1024
        ),
    )(activations, out_grad, weight)
    return tuple(
        pl.pallas_call(
            hand_over,
            out_shape=(
                jax.ShapeDtypeStruct((8, 4, 4, 128), BF16),
                jax.ShapeDtypeStruct((27, 32, 64), F32),
            ),
            in_specs=[hbm, hbm],
            out_specs=(hbm, hbm),
            scratch_shapes=[pltpu.VMEM((8, 4, 4, 128), BF16), pltpu.VMEM((27, 32, 64), F32), dma((4,))],
        )(gi, gw)
    )


def solution(mesh):
    ns = mesh.shape["space"]
    nz = 8 if ns % 8 == 0 else 2
    sizes = (ns // nz, nz, mesh.shape["chan"] // 2, mesh.shape["filt"])
    return jax.shard_map(
        functools.partial(body, sizes),
        mesh=mesh,
        in_specs=(
            P("chan", "space", None, None),
            P("filt", "chan", "space", None, None),
            P(None, "chan", "filt"),
        ),
        out_specs=(P(("chan", "filt"), "space", None, None), P(None, "chan", "filt")),
        check_vma=False,
    )
```

```python
import functools
import math

import jax
import jax.numpy as jnp
from jax import lax
from jax.experimental import pallas as pl
from jax.experimental.pallas import tpu as pltpu
from jax.sharding import PartitionSpec as P

MESH = pl.DeviceIdType.MESH
F32, BF16 = jnp.float32, jnp.bfloat16
ROWS = 512
TAP_ROWS = 128


def kernel(
    sizes, scale,
    act_hbm, shard_hbm, weight_hbm,
    gi_ref, gw_hbm,
    gw_ref,    act_raw, shard_raw, weight_raw, act_stage, shard_stage, shard_ref, taps_ref, in_sems, told,
    grads, acts, wparts, lhs, late, acc, mine, from_y, for_z, from_z, total, prod, outs, halo,
    s_own, r_own, s_act, r_act, s_filt, r_filt, s_wf, r_wf, s_wy, r_wy, s_pass, r_pass, s_edge, r_edge, s_pe, r_pe,
    s_yr, r_yr, s_zr, r_zr, s_zg, r_zg, s_yg, r_yg, s_halo, r_halo,
):
    ny, nz, nx, nf = sizes
    nc, ns = nx * 2, ny * nz
    space, chan, filt = lax.axis_index("space"), lax.axis_index("chan"), lax.axis_index("filt")
    row, run = space // nz, space % nz
    chip, core = chan // 2, chan % 2
    shard_rows = shard_ref.shape[0]
    own_filt = shard_rows // 16
    y_rows = ROWS // ny
    z_rows = y_rows // nz
    w_rows = TAP_ROWS // (2 * ny)
    layer_rows = 4 * own_filt
    inner_rows = pl.ds(layer_rows, 4 * layer_rows)
    w_mine = row * 2 + run % 2
    before, after = (space + ns - 1) % ns, (space + 1) % ns
    at_low, at_high = run == 0, run == nz - 1
    at_end = jnp.logical_or(at_low, at_high)
    across = jnp.where(at_low, before, after)
    edge_from = jnp.where(at_low, 0, 3)
    edge_to = jnp.where(at_low, 5, 0)
    edge_in = jnp.where(at_low, 0, 5)

    def layers(x):
        return pl.ds(pl.multiple_of(x * layer_rows, layer_rows), layer_rows)

    def at_y(d):
        return {"space": ((row + d) % ny) * nz + run}

    def at_z(d):
        return {"space": row * nz + (run + d) % nz}

    def at_w(e):
        return {"space": (row + e // 2) % ny * nz + (run + e % 2 - 2 * (e % 2) * (run % 2))}


    def filt_at(d):
        return (filt + d) % nf

    barrier = pltpu.get_barrier_semaphore()
    partners = [{"space": before}, {"space": after}]
    partners += [at_z(d) for d in (4, 3, 5, 2, 6, 1, 7) if d < nz]
    partners += [at_w(2 * e + 1) for e in range(1, ny)] + [at_y(d) for d in range(1, ny)]
    partners += [{"chan": (chan + d) % nc} for d in range(1, nc)]
    for partner in partners:
        pl.semaphore_signal(barrier, inc=1, device_id=partner, device_id_type=MESH)
    for d in range(1, nf):
        target = filt_at(d)

        @pl.when(filt < target)
        def _(target=target):
            pl.semaphore_signal(barrier, inc=1, device_id={"filt": target}, device_id_type=MESH)

            @pl.when(at_end)
            def _():
                where = {"filt": target, "space": across}
                pl.semaphore_signal(barrier, inc=1, device_id=where, device_id_type=MESH)

    loads = [
        pltpu.make_async_copy(src, dst, in_sems.at[n])
        for n, (src, dst) in enumerate(((shard_hbm, shard_raw), (act_hbm, act_raw), (weight_hbm, weight_raw)))
    ]
    for load in loads:
        load.start()

    sent = []

    def remote(src, dst, ssem, rsem, where, start=True, log=True):
        copy = pltpu.make_async_remote_copy(
            src_ref=src, dst_ref=dst, send_sem=ssem, recv_sem=rsem, device_id=where, device_id_type=MESH
        )
        if start:
            copy.start()
        if log:
            sent.append(copy)
        return copy

    lane = lax.broadcasted_iota(jnp.int32, (1, 128), 1)
    first, last = lane == 0, lane == 127
    loads[0].wait()
    for o in range(own_filt):
        shard_stage[:, :, o, :] = shard_raw[0, o].astype(F32)
    shard_ref[...] = shard_stage[...].reshape(shard_rows, 128).astype(BF16)
    grads[0, chan, inner_rows] = shard_ref[...]
    loads[1].wait()
    for i in range(32):
        act_stage[:, :, i, :] = act_raw[i].astype(F32)
    acts[1:5, 1:5] = act_stage[...].astype(BF16)
    empty = jnp.zeros((6, 32, 128), BF16)
    acts[:, 0] = empty
    acts[:, 5] = empty
    loads[2].wait()
    blank = jnp.zeros((8, 64), F32)
    for block in range(nf):
        pieces = []
        for k in range(0, 32, 2):
            pair = [
                weight_raw[t].astype(F32)[block * 8 : block * 8 + 8] if t < 27 else blank for t in (k, k + 1)
            ]
            pieces.append(jnp.concatenate(pair, axis=1))
        taps_ref[block] = jnp.concatenate(pieces, axis=0).astype(BF16)
    acc[...] = jnp.zeros(acc.shape, F32)
    pl.semaphore_wait(barrier, len(partners) + filt * jnp.where(at_end, 2, 1))

    over, wover, edge = {}, {}, {}
    for d in range(nf):
        target = filt_at(d)
        edge[d] = remote(
            shard_ref.at[layers(edge_from)], grads.at[d, chan, layers(edge_to)],
            s_edge.at[d], r_edge.at[d], {"filt": target, "space": across}, start=False, log=False,
        )
        if d > 0:
            over[d] = remote(
                shard_ref, grads.at[d, chan, inner_rows], s_filt.at[d - 1], r_filt.at[d - 1],
                {"filt": target}, start=False,
            )
            wover[d] = remote(
                taps_ref.at[target, pl.ds(pl.multiple_of(w_mine * w_rows, w_rows), w_rows)],
                wparts.at[w_mine, d - 1], s_wf.at[d - 1], r_wf.at[d - 1], {"filt": target}, start=False,
            )

    def send_over(d):
        wover[d].start()
        over[d].start()
        pl.when(at_end)(lambda: edge[d].start())

    def tell(d):
        target = filt_at(d)

        @pl.when(filt > target)
        def _():
            pl.semaphore_signal(told.at[d - 1, 0], inc=1, device_id={"filt": target}, device_id_type=MESH)

            @pl.when(at_end)
            def _():
                where = {"filt": target, "space": across}
                pl.semaphore_signal(told.at[d - 1, 1], inc=1, device_id=where, device_id_type=MESH)

    def send_back(d, who):
        pl.when(filt == who)(lambda: send_over(d))

    def send_on(d, who):
        @pl.when(functools.reduce(jnp.logical_or, [filt == w for w in who]))
        def _():
            pl.semaphore_wait(told.at[nf - d - 1, 0], 1)

            @pl.when(at_end)
            def _():
                pl.semaphore_wait(told.at[nf - d - 1, 1], 1)

            send_over(d)

    for d in (2, 1, 3):
        tell(d)
    for d in range(1, nf):
        send_back(d, nf - d)
    pl.when(at_end)(edge[0].start)
    own = [
        remote(
            shard_ref, grads.at[0, chan, inner_rows], s_own.at[d - 1], r_own.at[d - 1], {"chan": (chan + d) % nc}
        )
        for d in range(1, nc)
    ]
    up = remote(acts.at[4, pl.ds(1, 4)], acts.at[0, pl.ds(1, 4)], s_act.at[0], r_act.at[0], {"space": after})
    down = remote(acts.at[1, pl.ds(1, 4)], acts.at[5, pl.ds(1, 4)], s_act.at[1], r_act.at[1], {"space": before})

    rim = jnp.zeros((6, 256, 128), F32)
    for x in (0, 1, 6, 7):
        prod[x] = rim
    for x in range(2, 6):
        prod[x, 0] = rim[0]
        prod[x, 5] = rim[0]

    for copy in own:
        copy.wait_recv()
    up.wait_recv()
    down.wait_recv()
    zero = jnp.zeros((4, 32, 128), BF16)
    acts[0, 1:5] = jnp.where(space > 0, acts[0, 1:5], zero)
    acts[5, 1:5] = jnp.where(space < ns - 1, acts[5, 1:5], zero)

    def pair_of(block):
        parts = block.astype(F32).reshape(-1, 2, own_filt, 128)
        return [parts[:, i].reshape(-1, 128) for i in range(2)]

    def taps_step(h, carry):
        x, z = h // 2, (h % 2) * 2
        start = pl.multiple_of(h * 2 * own_filt, 2 * own_filt)
        columns = []
        for g in pair_of(grads[0, :, pl.ds(start + layer_rows, 2 * own_filt), :]):
            low = jnp.where(last, 0.0, pltpu.roll(g, 127, 1))
            high = jnp.where(first, 0.0, pltpu.roll(g, 1, 1))
            columns.append(jnp.concatenate([low, g, high], axis=0).astype(BF16))
        rhs = jnp.concatenate(columns, axis=1)
        halves = [
            jnp.concatenate([acts[x + a, z + c + i] for a in range(3) for c in range(3)], axis=0)
            for i in range(2)
        ]
        acc[:, 0:192] += lax.dot_general(
            jnp.concatenate(halves, axis=1), rhs, (((1,), (1,)), ((), ())), preferred_element_type=F32
        )
        return carry

    lax.fori_loop(0, 8, taps_step, 0)
    mine[0:288] = acc[:, 0:128] * scale
    third = acc[:, 128:256] * scale
    mine[288:432] = jnp.where(lane < 64, third[0:144], pltpu.roll(third[144:288], 64, 1))
    mine[432:512] = jnp.zeros((80, 128), F32)

    y_red = []
    for d in range(1, ny):
        theirs = pl.multiple_of((row + d) % ny * y_rows, y_rows)
        y_red.append(
            remote(mine.at[pl.ds(theirs, y_rows)], from_y.at[d - 1], s_yr.at[d - 1], r_yr.at[d - 1], at_y(d))
        )

    passed, passed_edge = {}, {}

    def pass_edge(d):
        for e in range(1, nc):
            block = grads.at[d, chan, layers(edge_in)]
            passed_edge[d, e] = remote(
                block, block, s_pe.at[d, e - 1], r_pe.at[d, e - 1], {"chan": (chan + e) % nc}, start=False, log=False
            )

        @pl.when(at_end)
        def _():
            edge[d].wait_recv()
            for e in range(1, nc):
                passed_edge[d, e].start()

    def forward(d):
        over[d].wait_recv()
        for e in range(1, nc):
            block = grads.at[d, chan, inner_rows]
            passed[d, e] = remote(
                block, block, s_pass.at[d - 1, e - 1], r_pass.at[d - 1, e - 1], {"chan": (chan + e) % nc}
            )
        pass_edge(d)

    def take(which):
        for (d, e), copy in passed.items():
            if d in which:
                copy.wait_recv()

        @pl.when(at_end)
        def _():
            for (d, e), copy in passed_edge.items():
                if d in which:
                    copy.wait_recv()

    for d, who in ((3, 2), (2, 3), (3, 3)):
        send_back(d, who)
    send_on(1, (1, 2))
    send_on(2, (1,))
    pass_edge(0)

    mine_y = pl.multiple_of(row * y_rows, y_rows)
    for copy in y_red:
        copy.wait_recv()
    part = mine[pl.ds(mine_y, y_rows)]
    for d in range(1, ny):
        part = part + from_y[d - 1]
    for_z[...] = part
    z_red = []
    for d in range(1, nz):
        theirs = pl.multiple_of((run + d) % nz * z_rows, z_rows)
        z_red.append(
            remote(for_z.at[pl.ds(theirs, z_rows)], from_z.at[d - 1], s_zr.at[d - 1], r_zr.at[d - 1], at_z(d))
        )

    send_on(1, (0,))
    send_on(3, (0,))
    wshare = {}

    def share_weights(d):
        wover[d].wait_recv()
        block = wparts.at[w_mine, d - 1]
        for e in range(1, 2 * ny):
            wshare[d, e] = remote(block, block, s_wy.at[d - 1, e - 1], r_wy.at[d - 1, e - 1], at_w(e))

    def widen(out, column, a, b):
        a = a.astype(F32)
        b = jnp.zeros_like(a) if b is None else b.astype(F32)
        columns = slice(column, column + 128)
        out[0:128, columns] = jnp.where(lane < 64, a, pltpu.roll(b, 64, 1)).astype(BF16)
        out[128:256, columns] = jnp.where(lane < 64, pltpu.roll(a, 64, 1), b).astype(BF16)

    forward(1)
    forward(3)

    for copy in z_red:
        copy.wait_recv()
    part = for_z[pl.ds(pl.multiple_of(run * z_rows, z_rows), z_rows)]
    for d in range(1, nz):
        part = part + from_z[d - 1]
    place = pl.ds(pl.multiple_of(mine_y + run * z_rows, z_rows), z_rows)
    total[place] = part
    z_gat = [
        remote(total.at[place], total.at[place], s_zg.at[d - 1], r_zg.at[d - 1], at_z(d)) for d in range(1, nz)
    ]
    send_on(2, (0,))
    share_weights(1)
    share_weights(3)
    share_weights(2)
    forward(2)
    for copy in z_gat:
        copy.wait_recv()
    place_y = pl.ds(mine_y, y_rows)
    y_gat = [
        remote(total.at[place_y], total.at[place_y], s_yg.at[d - 1], r_yg.at[d - 1], at_y(d)) for d in range(1, ny)
    ]

    for (d, e), copy in wshare.items():
        if d != 2:
            copy.wait_recv()
    widen(lhs, 0, taps_ref[filt], wparts[:, 0].reshape(TAP_ROWS, 128))
    widen(lhs, 128, wparts[:, 2].reshape(TAP_ROWS, 128), None)
    lowest = jnp.where(jnp.logical_and(at_low, space > 0), 0, 2)
    highest = jnp.where(jnp.logical_and(at_high, space < ns - 1), 12, 10)

    def product(which, left, add, steps):
        def step(h, carry):
            x, z = h // 2, (h % 2) * 2
            start = pl.multiple_of(h * 2 * own_filt, 2 * own_filt)
            parts = [pair_of(grads[d, :, pl.ds(start, 2 * own_filt), :]) for d in which]
            rhs = jnp.concatenate(
                [jnp.concatenate([p[i] for p in parts], axis=0) for i in range(2)], axis=1
            ).astype(BF16)
            result = jnp.dot(left[:, 0 : 64 * len(which)], rhs, preferred_element_type=F32)
            for i in range(2):
                half = result[:, i * 128 : i * 128 + 128]
                prod[x + 1, z + 1 + i] = prod[x + 1, z + 1 + i] + half if add else half
            return carry

        lax.fori_loop(*steps, step, 0)

    take((0, 1, 3))
    product((0, 1, 3), lhs, False, (lowest, highest))
    for (d, e), copy in wshare.items():
        if d == 2:
            copy.wait_recv()
    widen(late, 0, wparts[:, 1].reshape(TAP_ROWS, 128), None)
    take((2,))
    product((2,), late, True, (2, 4))
    product((2,), late, True, (8, 10))

    def sum_step(n, x):
        z = n
        sums = []
        for b in range(3):
            terms = []
            for a in range(3):
                for c in range(3):
                    k = (a * 3 + b) * 3 + c
                    at = (k % 2) * 128 + (k // 2) * 8
                    terms.append(prod[x + 2 - a, z + 2 - c, at : at + 8])
            sums.append(functools.reduce(jnp.add, terms))
        low = jnp.where(last, 0.0, pltpu.roll(sums[0], 127, 1))
        high = jnp.where(first, 0.0, pltpu.roll(sums[2], 1, 1))
        outs[x, z] = sums[1] + low + high
        return x

    def layer(x):
        for n in range(4):
            sum_step(n, x)

    low_out = remote(
        outs.at[0], halo.at[1], s_halo.at[0], r_halo.at[0], {"space": before}, start=False, log=False
    )
    high_out = remote(
        outs.at[5], halo.at[0], s_halo.at[1], r_halo.at[1], {"space": after}, start=False, log=False
    )

    @pl.when(jnp.logical_not(at_low))
    def _():
        layer(0)
        low_out.start()

    @pl.when(jnp.logical_not(at_high))
    def _():
        layer(5)
        high_out.start()

    for steps in ((lowest, 2), (4, 8), (10, highest)):
        product((2,), late, True, steps)

    def inner(x, carry):
        layer(x)
        return carry

    lax.fori_loop(1, 5, inner, 0)

    for copy in y_gat:
        copy.wait_recv()
    for a in range(3):
        for c in range(3):
            block = (a * 3 + c) * 32
            for b in range(2):
                gw_ref[(a * 3 + b) * 3 + c] = total[block : block + 32, b * 64 : b * 64 + 64]
            for half in range(2):
                at = block + half * 16
                left = 0 if at < 144 else 64
                src = 288 + (at if at < 144 else at - 144)
                gw_ref[(a * 3 + 2) * 3 + c, half * 16 : half * 16 + 16] = total[src : src + 16, left : left + 64]

    gw_store = pltpu.make_async_copy(gw_ref, gw_hbm, in_sems.at[3])
    gw_store.start()
    @pl.when(jnp.logical_not(at_low))
    def _():
        high_out.wait_recv()
        outs[1] = outs[1] + halo[0]
        low_out.wait_send()

    @pl.when(jnp.logical_not(at_high))
    def _():
        low_out.wait_recv()
        outs[4] = outs[4] + halo[1]
        high_out.wait_send()

    for i in range(8):
        gi_ref[i] = outs[1:5, :, i, :].astype(BF16)
    for copy in sent:
        copy.wait_send()
    gw_store.wait()

    @pl.when(at_end)
    def _():
        for copy in list(edge.values()) + list(passed_edge.values()):
            copy.wait_send()


def hand_over(gi_in, gw_in, gi_out, gw_out, gi_mid, gw_mid, sems):
    loads = [
        pltpu.make_async_copy(gw_in, gw_mid, sems.at[0]),
        pltpu.make_async_copy(gi_in, gi_mid, sems.at[1]),
    ]
    stores = [
        pltpu.make_async_copy(gw_mid, gw_out, sems.at[2]),
        pltpu.make_async_copy(gi_mid, gi_out, sems.at[3]),
    ]
    for load in loads:
        load.start()
    for load, store in zip(loads, stores):
        load.wait()
        store.start()
    for store in stores:
        store.wait()


def body(sizes, activations, out_grad, weight):
    ny, nz, nx, nf = sizes
    nc = nx * 2
    own_filt = out_grad.shape[1]
    cells = 16 * 128 * ny * nz
    dma = pltpu.SemaphoreType.DMA
    vmem = pl.BlockSpec(memory_space=pltpu.VMEM)
    hbm = pl.BlockSpec(memory_space=pl.ANY)
    y_rows = ROWS // ny
    z_rows = y_rows // nz
    pairs = []
    for shape in (
        (nc - 1,), (2,), (nf - 1,), (nf - 1,), (nf - 1, 2 * ny - 1), (nf - 1, nc - 1), (nf,), (nf, nc - 1),
        (ny - 1,), (nz - 1,), (nz - 1,), (ny - 1,), (2,),
    ):
        pairs += [dma(shape), dma(shape)]
    gi, gw = pl.pallas_call(
        functools.partial(kernel, sizes, 1.0 / math.sqrt(cells)),
        out_shape=(
            jax.ShapeDtypeStruct((8, 4, 4, 128), BF16),
            jax.ShapeDtypeStruct((27, 32, 64), F32),
        ),
        in_specs=[hbm] * 3,
        out_specs=(vmem, hbm),
        scratch_shapes=[
            pltpu.VMEM((27, 32, 64), F32),
            pltpu.VMEM(activations.shape, BF16),
            pltpu.VMEM(out_grad.shape, BF16),
            pltpu.VMEM(weight.shape, BF16),
            pltpu.VMEM((4, 4, 32, 128), F32),
            pltpu.VMEM((4, 4, own_filt, 128), F32),
            pltpu.VMEM((16 * own_filt, 128), BF16),
            pltpu.VMEM((nf, TAP_ROWS, 128), BF16),
            dma((4,)),
            pltpu.SemaphoreType.REGULAR((nf - 1, 2)),
            pltpu.VMEM((nf, nc, 24 * own_filt, 128), BF16),
            pltpu.VMEM((6, 6, 32, 128), BF16),
            pltpu.VMEM((2 * ny, nf - 1, TAP_ROWS // (2 * ny), 128), BF16),
            pltpu.VMEM((256, 256), BF16),
            pltpu.VMEM((256, 128), BF16),
            pltpu.VMEM((288, 256), F32),
            pltpu.VMEM((ROWS, 128), F32),
            pltpu.VMEM((ny - 1, y_rows, 128), F32),
            pltpu.VMEM((y_rows, 128), F32),
            pltpu.VMEM((nz - 1, z_rows, 128), F32),
            pltpu.VMEM((ROWS, 128), F32),
            pltpu.VMEM((8, 6, 256, 128), F32),
            pltpu.VMEM((6, 4, 8, 128), F32),
            pltpu.VMEM((2, 4, 8, 128), F32),
        ] + pairs,
        compiler_params=pltpu.CompilerParams(
            collective_id=0, has_side_effects=True, vmem_limit_bytes=63 * 1024 * 1024
        ),
    )(activations, out_grad, weight)
    return tuple(
        pl.pallas_call(
            hand_over,
            out_shape=(
                jax.ShapeDtypeStruct((8, 4, 4, 128), BF16),
                jax.ShapeDtypeStruct((27, 32, 64), F32),
            ),
            in_specs=[hbm, hbm],
            out_specs=(hbm, hbm),
            scratch_shapes=[pltpu.VMEM((8, 4, 4, 128), BF16), pltpu.VMEM((27, 32, 64), F32), dma((4,))],
        )(gi, gw)
    )


def solution(mesh):
    ns = mesh.shape["space"]
    nz = 8 if ns % 8 == 0 else 2
    sizes = (ns // nz, nz, mesh.shape["chan"] // 2, mesh.shape["filt"])
    return jax.shard_map(
        functools.partial(body, sizes),
        mesh=mesh,
        in_specs=(
            P("chan", "space", None, None),
            P("filt", "chan", "space", None, None),
            P(None, "chan", "filt"),
        ),
        out_specs=(P(("chan", "filt"), "space", None, None), P(None, "chan", "filt")),
        check_vma=False,
    )
```
